256 devices in a mesh: row: 64 (over y, z_lo, x), head: 4 (over z_hi, core).
Axes of the slice: x: 4, y: 4, z: 8 (z_hi: 2, z_lo: 4; z = z_hi * 4 + z_lo), core: 2. Of those that a mesh axis runs over, the one named last changes fastest.
Arguments:
- queries: bfloat16 [256, 1024, 4, 128], P('row', None, 'head'), may hold values from -40 to 40
- keys_proj: bfloat16 [256, 1024, 4, 128], P('row', None, 'head'), may hold values from -40 to 40
- values_proj: bfloat16 [256, 1024, 4, 128], P('row', None, 'head'), may hold values from -6 to 6
- grad_output: bfloat16 [256, 1024, 4, 128], P('row', None, 'head'), may hold values from -6 to 6
Outputs:
- attended: bfloat16 [256, 1024, 4, 128], P('row', 'head')
- grad_queries: bfloat16 [256, 1024, 4, 128], P('row', 'head')
- grad_keys: bfloat16 [256, 1024, 4, 128], P('row', 'head')
- grad_values: bfloat16 [256, 1024, 4, 128], P('row', 'head')
The draws below stay inside these ranges and needn't reach their ends.
All inputs are finite; a program needn't handle non-finite values.
Results may differ from the reference program's by a relative error of at most 0.024.
Values may be sent and summed in bfloat16 or wider, within the bound.
No kernel may reach another device: no remote copies, remote signals or barrier semaphores. Data moves between devices by JAX's collectives and lax.ppermute only.
A program may use at most 64 MiB of HBM per device.

```python
import jax
import jax.numpy as jnp
from jax import lax

HD = 128
COLS = 1024
ROWS = 256
HEADS = 4


def draw_queries(key, part):
    key = jax.random.fold_in(key, 11)
    values = jax.random.normal(key, (ROWS, COLS, HEADS, HD), jnp.float32)
    return values.astype(jnp.bfloat16)


def draw_keys_proj(key, part):
    key = jax.random.fold_in(key, 23)
    values = jax.random.normal(key, (ROWS, COLS, HEADS, HD), jnp.float32)
    return values.astype(jnp.bfloat16)


def block_levels(rng, dims, split, least, top_value):
    def one(axis_at, shards_of):
        draws = jax.random.uniform(jax.random.fold_in(jax.random.fold_in(rng, 6), axis_at), (shards_of,), jnp.float32, least / len(split), top_value / len(split))
        return jnp.repeat(jnp.exp(draws), dims[axis_at] // shards_of).reshape((-1,) + (1,) * (len(dims) - axis_at - 1))

    gain = one(*split[0])
    for cut in split[1:]:
        gain = gain * one(*cut)
    return gain


def bell_draw(own_key, extent, deviation, reach, pieces=(), kind=jnp.bfloat16):
    values = deviation * jax.random.normal(own_key, extent, jnp.float32)
    if pieces:
        values = values * block_levels(own_key, extent, pieces, -0.22, 0.18)
    return jnp.clip(values, -reach, reach).astype(kind)


def setup_inputs(seed: int = 0) -> dict:
    seeds = jax.random.split(jax.random.key(seed), 5)
    return {
        "queries": draw_queries(jax.random.fold_in(seeds[4], 71), 0),
        "keys_proj": draw_keys_proj(jax.random.fold_in(seeds[4], 71), 0),
        "values_proj": bell_draw(seeds[2], (ROWS, COLS, HEADS, HD), 1.0, 6.0, ((0, 64), (2, 4))),
        "grad_output": bell_draw(seeds[3], (ROWS, COLS, HEADS, HD), 1.0, 6.0, ((0, 64), (2, 4))),
    }


def attend(queries, keys_proj, values_proj, grad_output):
    count_rows = queries.shape[0]
    scale_factor = queries.shape[-1] ** -0.5
    scores = jnp.einsum("rbd,sbd->brs", queries.astype(jnp.float32), keys_proj.astype(jnp.float32)) * scale_factor
    causal = lax.broadcasted_iota(jnp.int32, (count_rows, count_rows), 1) <= lax.broadcasted_iota(jnp.int32, (count_rows, count_rows), 0)
    scores = jnp.where(causal[None], scores, -jnp.inf)
    largest = jnp.max(scores, axis=-1, keepdims=True)
    raw_weights = jnp.exp(scores - largest)
    weights = raw_weights / jnp.sum(raw_weights, axis=-1, keepdims=True)
    low_weights = weights.astype(jnp.bfloat16)
    attended = jnp.einsum("brs,sbd->rbd", low_weights.astype(jnp.float32), values_proj.astype(jnp.float32)).astype(jnp.bfloat16)
    row_dots = jnp.sum(grad_output.astype(jnp.float32) * attended.astype(jnp.float32), axis=-1)
    grad_weights = jnp.einsum("rbd,sbd->brs", grad_output.astype(jnp.float32), values_proj.astype(jnp.float32))
    grad_scores = (weights * (grad_weights - row_dots.T[:, :, None]) * scale_factor).astype(jnp.bfloat16)
    grad_values = jnp.einsum("brs,rbd->sbd", low_weights.astype(jnp.float32), grad_output.astype(jnp.float32)).astype(jnp.bfloat16)
    grad_queries = jnp.einsum("brs,sbd->rbd", grad_scores.astype(jnp.float32), keys_proj.astype(jnp.float32)).astype(jnp.bfloat16)
    grad_keys = jnp.einsum("brs,rbd->sbd", grad_scores.astype(jnp.float32), queries.astype(jnp.float32)).astype(jnp.bfloat16)
    return attended, grad_queries, grad_keys, grad_values


def reference(queries, keys_proj, values_proj, grad_output):
    count_rows, columns, heads_all, head_dim = queries.shape
    block_width = 128
    number = columns * heads_all // block_width

    def stacked(array):
        return array.reshape(count_rows, number, block_width, head_dim).transpose(1, 0, 2, 3)

    def unstacked(array):
        return array.transpose(1, 0, 2, 3).reshape(count_rows, columns, heads_all, head_dim)

    results = lax.map(lambda items: attend(items[0], items[1], items[2], items[3]),
                      (stacked(queries), stacked(keys_proj), stacked(values_proj), stacked(grad_output)))
    return (unstacked(results[0]), unstacked(results[1]), unstacked(results[2]), unstacked(results[3]))
```

```python
import jax
import jax.numpy as jnp
from jax import lax
from jax.experimental import pallas as pl
from jax.experimental.pallas import tpu as pltpu
from jax.sharding import PartitionSpec as P

NAMES = ("row", "head")
LAST = (((1,), (1,)), ((), ()))
FIRST = (((0,), (0,)), ((), ()))
F32 = jnp.float32
LIMIT = 48 * 2**20


def attend_column(query, key, value, cotangent):
    count = query.shape[0]
    scale = query.shape[-1] ** (-0.5)
    scores = lax.dot_general(key, query, LAST, preferred_element_type=F32)
    grad_weights = lax.dot_general(value, cotangent, LAST, preferred_element_type=F32)
    key_at = lax.broadcasted_iota(jnp.int32, (count, count), 0)
    query_at = lax.broadcasted_iota(jnp.int32, (count, count), 1)
    scores = jnp.where(key_at <= query_at, scores, -jnp.inf)
    largest = jnp.max(scores, axis=0, keepdims=True)
    raw = jnp.exp((scores - largest) * scale)
    weights = raw * (1.0 / jnp.sum(raw, axis=0, keepdims=True))
    dots = jnp.sum(weights * grad_weights, axis=0, keepdims=True)
    low = weights.astype(jnp.bfloat16)
    grad_scores = (weights * (grad_weights - dots) * scale).astype(jnp.bfloat16)
    return (
        lax.dot_general(low, value, FIRST, preferred_element_type=F32),
        lax.dot_general(grad_scores, key, FIRST, preferred_element_type=F32),
        jnp.dot(grad_scores, query, preferred_element_type=F32),
        jnp.dot(low, cotangent, preferred_element_type=F32),
    )


def pack_kernel(*refs):
    *in_refs, out_ref, sems = refs
    copies = []
    for array, ref in enumerate(in_refs):
        for row in range(ref.shape[0]):
            for part in range(ref.shape[1]):
                copies.append(
                    pltpu.make_async_copy(
                        ref.at[row, part], out_ref.at[:, array, row, part], sems.at[len(copies)]
                    )
                )
                copies[-1].start()
    for copy in copies:
        copy.wait()


def pack(arrays):
    row, part, owner, inner, feature = arrays[0].shape
    count = len(arrays)
    return pl.pallas_call(
        pack_kernel,
        out_shape=jax.ShapeDtypeStruct((owner, count, row, part, inner, feature), arrays[0].dtype),
        in_specs=[pl.BlockSpec(memory_space=pl.ANY)] * count,
        out_specs=pl.BlockSpec(memory_space=pl.ANY),
        scratch_shapes=[pltpu.SemaphoreType.DMA((count * row * part,))],
        name="pack",
    )(*arrays)


def attend_kernel(in_ref, out_ref, wide_in, wide_out):
    sources, arrays, row, columns, feature = in_ref.shape
    owners, parts, _, _, inner, _ = out_ref.shape
    rows = sources * row

    def widen(source, carry):
        for array in range(arrays):
            block = in_ref[source, array].reshape(row * columns, feature)
            start = pl.multiple_of(source * row * columns, row * columns)
            wide_in[array, pl.ds(start, row * columns), :] = block.astype(F32)
        return carry

    lax.fori_loop(0, sources, widen, 0)

    def column(at, carry):
        block = [
            wide_in[array, pl.ds(at, rows, stride=columns), :].astype(jnp.bfloat16)
            for array in range(arrays)
        ]
        for array, result in enumerate(attend_column(*block)):
            wide_out[array, pl.ds(at, rows, stride=columns), :] = result
        return carry

    lax.fori_loop(0, columns, column, 0)

    def narrow(owner, carry):
        for array in range(arrays):
            for r in range(row):
                for part in range(parts):
                    start = owner * row * columns + r * columns + part * inner
                    out_ref[owner, part, array, r] = wide_out[array, pl.ds(start, inner), :].astype(
                        out_ref.dtype
                    )
        return carry

    lax.fori_loop(0, owners, narrow, 0)


def attend(arrived, parts):
    sources, arrays, row, columns, feature = arrived.shape
    rows = sources * row
    whole = pl.BlockSpec(memory_space=pltpu.VMEM)
    return pl.pallas_call(
        attend_kernel,
        out_shape=jax.ShapeDtypeStruct(
            (sources, parts, arrays, row, columns // parts, feature), arrived.dtype
        ),
        in_specs=[whole],
        out_specs=whole,
        scratch_shapes=[pltpu.VMEM((arrays, rows * columns, feature), F32)] * 2,
        compiler_params=pltpu.CompilerParams(vmem_limit_bytes=LIMIT),
        cost_estimate=pl.CostEstimate(
            flops=12 * columns * rows * rows * feature,
            bytes_accessed=4 * arrived.size,
            transcendentals=columns * rows * rows,
        ),
        name="attend",
    )(arrived)


def unpack_kernel(in_ref, *refs):
    *out_refs, wide = refs
    sources, heads, arrays, rows, inner, feature = in_ref.shape

    def step(source, carry):
        for array in range(arrays):
            for row in range(rows):
                base = (array * rows + row) * heads * inner
                for head in range(heads):
                    wide[pl.ds(base + head * inner, inner), :] = in_ref[
                        source, head, array, row
                    ].astype(F32)
                for at in range(inner):
                    out_refs[array][row, source * inner + at] = wide[
                        pl.ds(base + at, heads, stride=inner), :
                    ].astype(in_ref.dtype)
        return carry

    lax.fori_loop(0, sources, step, 0)


def unpack(returned):
    sources, heads, arrays, rows, inner, feature = returned.shape
    whole = pl.BlockSpec(memory_space=pltpu.VMEM)
    return pl.pallas_call(
        unpack_kernel,
        out_shape=[jax.ShapeDtypeStruct((rows, sources * inner, heads, feature), returned.dtype)]
        * arrays,
        in_specs=[whole],
        out_specs=[whole] * arrays,
        scratch_shapes=[pltpu.VMEM((arrays * rows * heads * inner, feature), F32)],
        compiler_params=pltpu.CompilerParams(vmem_limit_bytes=LIMIT),
        name="unpack",
    )(returned)


def shards(*arrays):
    row_devs = lax.axis_size("row")
    head_devs = lax.axis_size("head")
    local_rows, columns, _, features = arrays[0].shape
    inner = columns // (row_devs * head_devs)
    count = len(arrays)

    packed = pack([a.reshape(local_rows, head_devs, row_devs, inner, features) for a in arrays])
    packed = packed.reshape(row_devs, count, local_rows, head_devs * inner, features)
    arrived = lax.all_to_all(packed, "row", 0, 0, tiled=True)
    results = attend(arrived, head_devs)
    results = results.reshape(row_devs * head_devs, count, local_rows, inner, features)
    returned = lax.all_to_all(results, NAMES, 0, 0, tiled=True)
    returned = returned.reshape(row_devs, head_devs, count, local_rows, inner, features)
    return tuple(unpack(returned))


def solution(mesh):
    spec_in = P("row", None, "head", None)
    spec_out = P("row", "head", None, None)
    return jax.shard_map(
        shards, mesh=mesh, in_specs=(spec_in,) * 4, out_specs=(spec_out,) * 4, check_vma=False
    )
```

```python
import jax
import jax.numpy as jnp
from jax import lax
from jax.experimental import pallas as pl
from jax.experimental.pallas import tpu as pltpu
from jax.sharding import PartitionSpec as P

NAMES = ("row", "head")
LAST = (((1,), (1,)), ((), ()))
FIRST = (((0,), (0,)), ((), ()))
F32 = jnp.float32
LIMIT = 48 * 2**20


def attend_column(query, key, value, cotangent):
    count = query.shape[0]
    scale = query.shape[-1] ** (-0.5)
    scores = lax.dot_general(key, query, LAST, preferred_element_type=F32)
    grad_weights = lax.dot_general(value, cotangent, LAST, preferred_element_type=F32)
    key_at = lax.broadcasted_iota(jnp.int32, (count, count), 0)
    query_at = lax.broadcasted_iota(jnp.int32, (count, count), 1)
    scores = jnp.where(key_at <= query_at, scores, -jnp.inf)
    largest = jnp.max(scores, axis=0, keepdims=True)
    raw = jnp.exp((scores - largest) * scale)
    weights = raw * (1.0 / jnp.sum(raw, axis=0, keepdims=True))
    dots = jnp.sum(weights * grad_weights, axis=0, keepdims=True)
    low = weights.astype(jnp.bfloat16)
    grad_scores = (weights * (grad_weights - dots) * scale).astype(jnp.bfloat16)
    return (
        lax.dot_general(low, value, FIRST, preferred_element_type=F32),
        lax.dot_general(grad_scores, key, FIRST, preferred_element_type=F32),
        jnp.dot(grad_scores, query, preferred_element_type=F32),
        jnp.dot(low, cotangent, preferred_element_type=F32),
    )


def pack_kernel(*refs):
    *in_refs, out_ref = refs
    rows, parts, owners, _, _ = in_refs[0].shape

    def step(owner, carry):
        for array, ref in enumerate(in_refs):
            for row in range(rows):
                for part in range(parts):
                    out_ref[owner, array, row, part] = ref[row, part, owner]
        return carry

    lax.fori_loop(0, owners, step, 0)


def pack(arrays):
    row, part, owner, inner, feature = arrays[0].shape
    count = len(arrays)
    whole = pl.BlockSpec(memory_space=pltpu.VMEM)
    return pl.pallas_call(
        pack_kernel,
        out_shape=jax.ShapeDtypeStruct((owner, count, row, part, inner, feature), arrays[0].dtype),
        in_specs=[whole] * count,
        out_specs=whole,
        compiler_params=pltpu.CompilerParams(vmem_limit_bytes=LIMIT),
        name="pack",
    )(*arrays)


def attend_kernel(in_ref, out_ref, wide_in, wide_out):
    sources, arrays, row, columns, feature = in_ref.shape
    owners, parts, _, _, inner, _ = out_ref.shape
    rows = sources * row

    def widen(source, carry):
        for array in range(arrays):
            block = in_ref[source, array].reshape(row * columns, feature)
            start = pl.multiple_of(source * row * columns, row * columns)
            wide_in[array, pl.ds(start, row * columns), :] = block.astype(F32)
        return carry

    lax.fori_loop(0, sources, widen, 0)

    def column(at, carry):
        block = [
            wide_in[array, pl.ds(at, rows, stride=columns), :].astype(jnp.bfloat16)
            for array in range(arrays)
        ]
        for array, result in enumerate(attend_column(*block)):
            wide_out[array, pl.ds(at, rows, stride=columns), :] = result
        return carry

    lax.fori_loop(0, columns, column, 0)

    def narrow(owner, carry):
        for array in range(arrays):
            for r in range(row):
                for part in range(parts):
                    start = owner * row * columns + r * columns + part * inner
                    out_ref[owner, part, array, r] = wide_out[array, pl.ds(start, inner), :].astype(
                        out_ref.dtype
                    )
        return carry

    lax.fori_loop(0, owners, narrow, 0)


def attend(arrived, parts):
    sources, arrays, row, columns, feature = arrived.shape
    rows = sources * row
    whole = pl.BlockSpec(memory_space=pltpu.VMEM)
    return pl.pallas_call(
        attend_kernel,
        out_shape=jax.ShapeDtypeStruct(
            (sources, parts, arrays, row, columns // parts, feature), arrived.dtype
        ),
        in_specs=[whole],
        out_specs=whole,
        scratch_shapes=[pltpu.VMEM((arrays, rows * columns, feature), F32)] * 2,
        compiler_params=pltpu.CompilerParams(vmem_limit_bytes=LIMIT),
        cost_estimate=pl.CostEstimate(
            flops=12 * columns * rows * rows * feature,
            bytes_accessed=4 * arrived.size,
            transcendentals=columns * rows * rows,
        ),
        name="attend",
    )(arrived)


def unpack_kernel(in_ref, *refs):
    *out_refs, wide = refs
    sources, heads, arrays, rows, inner, feature = in_ref.shape

    def step(source, carry):
        for array in range(arrays):
            for row in range(rows):
                base = (array * rows + row) * heads * inner
                for head in range(heads):
                    wide[pl.ds(base + head * inner, inner), :] = in_ref[
                        source, head, array, row
                    ].astype(F32)
                for at in range(inner):
                    out_refs[array][row, source * inner + at] = wide[
                        pl.ds(base + at, heads, stride=inner), :
                    ].astype(in_ref.dtype)
        return carry

    lax.fori_loop(0, sources, step, 0)


def unpack(returned):
    sources, heads, arrays, rows, inner, feature = returned.shape
    whole = pl.BlockSpec(memory_space=pltpu.VMEM)
    return pl.pallas_call(
        unpack_kernel,
        out_shape=[jax.ShapeDtypeStruct((rows, sources * inner, heads, feature), returned.dtype)]
        * arrays,
        in_specs=[whole],
        out_specs=[whole] * arrays,
        scratch_shapes=[pltpu.VMEM((arrays * rows * heads * inner, feature), F32)],
        compiler_params=pltpu.CompilerParams(vmem_limit_bytes=LIMIT),
        name="unpack",
    )(returned)


def shards(*arrays):
    row_devs = lax.axis_size("row")
    head_devs = lax.axis_size("head")
    local_rows, columns, _, features = arrays[0].shape
    inner = columns // (row_devs * head_devs)
    count = len(arrays)

    packed = pack([a.reshape(local_rows, head_devs, row_devs, inner, features) for a in arrays])
    packed = packed.reshape(row_devs, count, local_rows, head_devs * inner, features)
    arrived = lax.all_to_all(packed, "row", 0, 0, tiled=True)
    results = attend(arrived, head_devs)
    results = results.reshape(row_devs * head_devs, count, local_rows, inner, features)
    returned = lax.all_to_all(results, NAMES, 0, 0, tiled=True)
    returned = returned.reshape(row_devs, head_devs, count, local_rows, inner, features)
    return tuple(unpack(returned))


def solution(mesh):
    spec_in = P("row", None, "head", None)
    spec_out = P("row", "head", None, None)
    return jax.shard_map(
        shards, mesh=mesh, in_specs=(spec_in,) * 4, out_specs=(spec_out,) * 4, check_vma=False
    )
```

```python
import jax
import jax.numpy as jnp
from jax import lax
from jax.experimental import pallas as pl
from jax.experimental.pallas import tpu as pltpu
from jax.sharding import Mesh, PartitionSpec as P

FINE = ("y", "z", "x", "w", "core")
SIZES = (4, 4, 4, 2, 2)
LAST = (((1,), (1,)), ((), ()))
FIRST = (((0,), (0,)), ((), ()))
F32 = jnp.float32
BF16 = jnp.bfloat16
LIMIT = 48 * 2**20
WHOLE = pl.BlockSpec(memory_space=pltpu.VMEM)


def edge(z, count):
    return jnp.where((z == 0) | (z == count - 1), 1, 0)


def other_run(w, chunk, z, count):
    return (w + chunk + edge(z, count)) % 2


def attend_column(query, key, value, cotangent):
    count = query.shape[0]
    scale = query.shape[-1] ** (-0.5)
    scores = lax.dot_general(key, query, LAST, preferred_element_type=F32)
    grad_weights = lax.dot_general(value, cotangent, LAST, preferred_element_type=F32)
    key_at = lax.broadcasted_iota(jnp.int32, (count, count), 0)
    query_at = lax.broadcasted_iota(jnp.int32, (count, count), 1)
    scores = jnp.where(key_at <= query_at, scores, -jnp.inf)
    largest = jnp.max(scores, axis=0, keepdims=True)
    raw = jnp.exp((scores - largest) * scale)
    weights = raw * (1.0 / jnp.sum(raw, axis=0, keepdims=True))
    dots = jnp.sum(weights * grad_weights, axis=0, keepdims=True)
    low = weights.astype(BF16)
    grad_scores = (weights * (grad_weights - dots) * scale).astype(BF16)
    return (
        lax.dot_general(low, value, FIRST, preferred_element_type=F32),
        lax.dot_general(grad_scores, key, FIRST, preferred_element_type=F32),
        jnp.dot(grad_scores, query, preferred_element_type=F32),
        jnp.dot(low, cotangent, preferred_element_type=F32),
    )


def pack_kernel(sizes, chunk, split, place_ref, *refs):
    ys, zs, xs, _, cores = sizes
    in_refs, out_refs = refs[:4], refs[4:]
    rows = in_refs[0].shape[0]
    my_z, my_w = place_ref[0], place_ref[1]
    for shift in range(zs):
        z = (my_z + shift) % zs
        run = other_run(my_w, chunk, z, zs)

        def step(at, carry, shift=shift, z=z, run=run):
            y, x = at // xs, at % xs
            owner = (y * zs + z) * xs + x
            for core in range(cores):
                for array, ref in enumerate(in_refs):
                    for row in range(rows):
                        tile = ref[row, run * cores + core, owner]
                        if split:
                            out_refs[shift][at * cores + core, array, row] = tile
                        else:
                            out_refs[0][at * cores + core, shift, array, row] = tile
            return carry

        lax.fori_loop(0, ys * xs, step, 0)


def pack(arrays, place, sizes, chunk, split):
    ys, zs, xs, _, cores = sizes
    rows, _, _, inner, feature = arrays[0].shape
    tail = (len(arrays), rows, inner, feature)
    if split:
        shapes = [jax.ShapeDtypeStruct((ys * xs * cores, *tail), BF16)] * zs
    else:
        shapes = [jax.ShapeDtypeStruct((ys * xs * cores, zs, *tail), BF16)]
    return pl.pallas_call(
        lambda *refs: pack_kernel(sizes, chunk, split, *refs),
        out_shape=shapes,
        in_specs=[pl.BlockSpec(memory_space=pltpu.SMEM)] + [WHOLE] * 4,
        out_specs=[WHOLE] * len(shapes),
        compiler_params=pltpu.CompilerParams(vmem_limit_bytes=LIMIT),
        name="pack",
    )(place, *arrays)


def attend_kernel(sizes, joined, split, place_ref, *refs):
    ys, zs, xs, _, cores = sizes
    in_refs, refs = (refs[:1], refs[1:]) if joined else (refs[:zs], refs[zs:])
    *out_refs, wide_in, wide_out = refs
    arrays, tile, feature = in_refs[0].shape[-3:]
    local = 4
    inner = tile // local
    rows = ys * zs * xs * local
    my_z = place_ref[0]
    for shift in range(zs):
        z = (my_z - shift + zs) % zs

        def widen(at, carry, shift=shift, z=z):
            y, x = at // xs, at % xs
            start = ((y * zs + z) * xs + x) * tile
            for core in range(cores):
                for array in range(arrays):
                    source = at * cores + core
                    block = in_refs[0][source, shift, array] if joined else in_refs[shift][source, array]
                    to = pl.multiple_of(core * rows * inner + start, tile)
                    wide_in[array, pl.ds(to, tile), :] = block.astype(F32)
            return carry

        lax.fori_loop(0, ys * xs, widen, 0)

    def column(at, carry):
        core, place = at // inner, at % inner
        block = [
            wide_in[array, pl.ds(core * rows * inner + place, rows, stride=inner), :].astype(BF16)
            for array in range(arrays)
        ]
        for array, result in enumerate(attend_column(*block)):
            wide_out[array, pl.ds(place * cores + core, rows, stride=inner * cores), :] = result
        return carry

    lax.fori_loop(0, cores * inner, column, 0)

    for shift in range(zs):
        z = (my_z + shift) % zs

        def narrow(at, carry, shift=shift, z=z):
            y, x = at // xs, at % xs
            start = pl.multiple_of(((y * zs + z) * xs + x) * tile * cores, tile * cores)
            for array in range(arrays):
                block = wide_out[array, pl.ds(start, tile * cores), :].astype(BF16)
                if split:
                    out_refs[shift][at, array] = block
                else:
                    out_refs[0][at, shift, array] = block
            return carry

        lax.fori_loop(0, ys * xs, narrow, 0)


def attend(pieces, place, sizes, joined, split):
    ys, zs, xs, _, cores = sizes
    arrays, tile, feature = pieces[0].shape[-3:]
    rows = ys * zs * xs * 4
    columns = tile // 4 * cores
    tail = (arrays, tile * cores, feature)
    if split:
        shapes = [jax.ShapeDtypeStruct((ys * xs, *tail), BF16)] * zs
    else:
        shapes = [jax.ShapeDtypeStruct((ys * xs, zs, *tail), BF16)]
    return pl.pallas_call(
        lambda *refs: attend_kernel(sizes, joined, split, *refs),
        out_shape=shapes,
        in_specs=[pl.BlockSpec(memory_space=pltpu.SMEM)] + [WHOLE] * len(pieces),
        out_specs=[WHOLE] * len(shapes),
        scratch_shapes=[pltpu.VMEM((arrays, rows * columns, feature), F32)] * 2,
        compiler_params=pltpu.CompilerParams(vmem_limit_bytes=LIMIT),
        cost_estimate=pl.CostEstimate(
            flops=12 * columns * rows * rows * feature,
            bytes_accessed=4 * arrays * rows * columns * feature,
            transcendentals=columns * rows * rows,
        ),
        name="attend",
    )(place, *pieces)


def join_kernel(*refs):
    *in_refs, out_ref = refs
    for shift, ref in enumerate(in_refs):
        out_ref[:, shift] = ref[...]


def join(pieces):
    first, *tail = pieces[0].shape
    return pl.pallas_call(
        join_kernel,
        out_shape=jax.ShapeDtypeStruct((first, len(pieces), *tail), BF16),
        in_specs=[WHOLE] * len(pieces),
        out_specs=WHOLE,
        compiler_params=pltpu.CompilerParams(vmem_limit_bytes=LIMIT),
        name="join",
    )(*pieces)


def part_kernel(in_ref, *out_refs):
    for shift, ref in enumerate(out_refs):
        ref[...] = in_ref[:, shift]


def part(joined):
    first, shifts, *tail = joined.shape
    return pl.pallas_call(
        part_kernel,
        out_shape=[jax.ShapeDtypeStruct((first, *tail), BF16)] * shifts,
        in_specs=[WHOLE],
        out_specs=[WHOLE] * shifts,
        compiler_params=pltpu.CompilerParams(vmem_limit_bytes=LIMIT),
        name="part",
    )(joined)


def unpack_kernel(sizes, place_ref, first_ref, *refs):
    ys, zs, xs, ws, cores = sizes
    second_refs, refs = refs[:zs], refs[zs:]
    *out_refs, narrow_in, wide = refs
    arrays, tile, feature = first_ref.shape[-3:]
    rows, width, _ = out_refs[0].shape
    heads = ws * cores
    inner = tile // cores // rows
    my_z, my_w = place_ref[0], place_ref[1]
    for shift in range(zs):
        z = (my_z - shift + zs) % zs
        runs = [other_run(my_w, chunk, z, zs) for chunk in range(2)]

        def step(at, carry, shift=shift, z=z, runs=runs):
            y, x = at // xs, at % xs
            owner = (y * zs + z) * xs + x
            for array in range(arrays):
                for chunk in range(2):
                    block = first_ref[at, shift, array] if chunk == 0 else second_refs[shift][at, array]
                    spot = (array * 2 + chunk) * tile
                    narrow_in[pl.ds(spot, tile), :] = block.astype(F32)
                    for core in range(cores):
                        to = array * tile * ws + runs[chunk] * cores + core
                        wide[pl.ds(to, tile // cores, stride=heads), :] = narrow_in[
                            pl.ds(spot + core, tile // cores, stride=cores), :
                        ]
                for row in range(rows):
                    size = inner * heads
                    block = wide[pl.ds(array * tile * ws + row * size, size), :].astype(BF16)
                    to = pl.multiple_of(owner * size, size)
                    out_refs[array][row, pl.ds(to, size), :] = block
            return carry

        lax.fori_loop(0, ys * xs, step, 0)


def unpack(first, second, place, sizes, rows):
    ys, zs, xs, ws, cores = sizes
    arrays, tile, feature = first.shape[-3:]
    inner = tile // cores // rows
    width = ys * zs * xs * inner * ws * cores
    return pl.pallas_call(
        lambda *refs: unpack_kernel(sizes, *refs),
        out_shape=[jax.ShapeDtypeStruct((rows, width, feature), BF16)] * arrays,
        in_specs=[pl.BlockSpec(memory_space=pltpu.SMEM)] + [WHOLE] * (1 + zs),
        out_specs=[WHOLE] * arrays,
        scratch_shapes=[
            pltpu.VMEM((arrays * tile * 2, feature), F32),
            pltpu.VMEM((arrays * tile * ws, feature), F32),
        ],
        compiler_params=pltpu.CompilerParams(vmem_limit_bytes=LIMIT),
        name="unpack",
    )(place, first, *second)


def z_in(pieces, zs):
    return [pieces[0]] + [
        lax.ppermute(pieces[k], "z", [(z, (z + k) % zs) for z in range(zs)]) for k in range(1, zs)
    ]


def z_out(pieces, zs, ws, chunk):
    def pairs(k):
        made = []
        for z in range(zs):
            for w in range(ws):
                to = (w + chunk + (z in (0, zs - 1))) % ws
                made.append((z * ws + w, (z + k) % zs * ws + to))
        return made

    return [lax.ppermute(pieces[k], ("z", "w"), pairs(k)) for k in range(zs)]


def shards(*arrays):
    sizes = tuple(lax.axis_size(name) for name in FINE)
    ys, zs, xs, ws, cores = sizes
    rows, columns, _, feature = arrays[0].shape
    owners = ys * zs * xs
    inner = columns // (owners * ws * cores)
    arrays = [a.reshape(rows, ws * cores, owners, inner, feature) for a in arrays]
    place = jnp.stack([lax.axis_index("z"), lax.axis_index("w")]).astype(jnp.int32)

    def flat(piece):
        return piece.reshape(*piece.shape[:-3], rows * inner, feature)

    def across(whole, names):
        return lax.all_to_all(whole, names, 0, 0, tiled=True)

    first = z_in([flat(p) for p in pack(arrays, place, sizes, 0, True)], zs)
    second = across(flat(pack(arrays, place, sizes, 1, False)[0]), ("y", "x", "core"))
    second = z_in(part(second), zs)
    first = across(join(first), ("y", "x", "core"))

    first = attend([first], place, sizes, True, True)
    first = z_out(first, zs, ws, 0)
    second = attend(second, place, sizes, False, False)[0]
    second = z_out(part(across(second, ("y", "x"))), zs, ws, 1)
    first = across(join(first), ("y", "x"))

    results = unpack(first, second, place, sizes, rows)
    return tuple(r.reshape(rows, columns // (ws * cores), ws * cores, feature) for r in results)


def solution(mesh):
    fine = Mesh(mesh.devices.reshape(SIZES), FINE)
    row, head = FINE[:3], FINE[3:]
    spec_in = P(row, None, head, None)
    spec_out = P(row, head, None, None)
    return jax.shard_map(
        shards, mesh=fine, in_specs=(spec_in,) * 4, out_specs=(spec_out,) * 4, check_vma=False
    )
```

```python
import jax
import jax.numpy as jnp
from jax import lax
from jax.experimental import pallas as pl
from jax.experimental.pallas import tpu as pltpu
from jax.sharding import PartitionSpec as P

NAMES = ("row", "head")
LAST = (((1,), (1,)), ((), ()))
FIRST = (((0,), (0,)), ((), ()))
F32 = jnp.float32
BF16 = jnp.bfloat16
LIMIT = 48 * 2**20
ALL = 58 * 2**20
LOG2E = 1.4426950408889634
FAR = pl.BlockSpec(memory_space=pltpu.HBM)
WHOLE = pl.BlockSpec(memory_space=pltpu.VMEM)


def dot(a, b, dims):
    return lax.dot_general(a, b, dims, preferred_element_type=F32)


def attend_column(query, key, value, cotangent):
    half = query.shape[0] // 2
    scale = query.shape[-1] ** (-0.5)
    causal = lax.broadcasted_iota(jnp.int32, (half, half), 0) <= lax.broadcasted_iota(
        jnp.int32, (half, half), 1
    )
    lows, grads = [], []
    for at in range(2):
        mine, keys = slice(at * half, (at + 1) * half), slice(0, (at + 1) * half)
        scores = dot(key[keys], query[mine], LAST) * (scale * LOG2E)
        grad_weights = dot(value[keys], cotangent[mine], LAST)
        diagonal = jnp.where(causal, scores[mine], -jnp.inf)
        scores = jnp.concatenate([scores[:half], diagonal], 0) if at else diagonal
        raw = jnp.exp2(scores - jnp.max(scores, axis=0, keepdims=True))
        weights = raw * (1.0 / jnp.sum(raw, axis=0, keepdims=True))
        dots = jnp.sum(weights * grad_weights, axis=0, keepdims=True)
        lows.append(weights.astype(BF16))
        grads.append(((grad_weights - dots) * (weights * scale)).astype(BF16))

    def to_queries(parts, other):
        return jnp.concatenate(
            [dot(parts[0], other[:half], FIRST), dot(parts[1], other, FIRST)], axis=0
        )

    def to_keys(parts, other):
        upper = jnp.concatenate([parts[0], jnp.zeros((half, half), BF16)], axis=0)
        both = jnp.concatenate([upper, parts[1]], axis=1)
        return jnp.dot(both, other, preferred_element_type=F32)

    return (
        to_queries(lows, value),
        to_queries(grads, key),
        to_keys(grads, query),
        to_keys(lows, cotangent),
    )


def pack_kernel(*refs):
    *far_refs, out_ref, held, sems = refs
    rows, parts, owners, _, _ = far_refs[0].shape
    copies = [
        [
            pltpu.make_async_copy(ref.at[row], held.at[array, row], sems.at[array, row])
            for array, ref in enumerate(far_refs)
        ]
        for row in range(rows)
    ]
    for some in copies:
        for copy in some:
            copy.start()
    for row in range(rows):
        for copy in copies[row]:
            copy.wait()

        def step(owner, carry, row=row):
            for array in range(len(far_refs)):
                for part in range(parts):
                    out_ref[owner, array, row, part] = held[array, row, part, owner]
            return carry

        lax.fori_loop(0, owners, step, 0, unroll=2)


def pack(arrays):
    row, part, owner, inner, feature = arrays[0].shape
    count = len(arrays)
    return pl.pallas_call(
        pack_kernel,
        out_shape=jax.ShapeDtypeStruct((owner, count, row, part, inner, feature), BF16),
        in_specs=[FAR] * count,
        out_specs=WHOLE,
        scratch_shapes=[
            pltpu.VMEM((count, *arrays[0].shape), BF16),
            pltpu.SemaphoreType.DMA((count, row)),
        ],
        compiler_params=pltpu.CompilerParams(vmem_limit_bytes=ALL),
        name="pack",
    )(*arrays)


def attend_kernel(together, in_ref, out_ref, wide_in, wide_out):
    sources, arrays, row, columns, feature = in_ref.shape
    owners, parts, _, tile, _ = out_ref.shape
    inner = tile // row
    rows = sources * row

    def widen(source, carry):
        for array in range(arrays):
            block = in_ref[source, array].reshape(row * columns, feature)
            start = pl.multiple_of(source * row * columns, row * columns)
            wide_in[array, pl.ds(start, row * columns), :] = block.astype(F32)
        return carry

    lax.fori_loop(0, sources, widen, 0, unroll=2)

    def step(at, carry):
        for place in range(together):
            column = at * together + place
            block = [
                wide_in[array, pl.ds(column, rows, stride=columns), :].astype(BF16)
                for array in range(arrays)
            ]
            start = (column // inner) * rows * inner + column % inner
            for array, result in enumerate(attend_column(*block)):
                wide_out[array, pl.ds(start, rows, stride=inner), :] = result
        return carry

    lax.fori_loop(0, columns // together, step, 0)

    def narrow(owner, carry):
        for array in range(arrays):
            for part in range(parts):
                start = pl.multiple_of(part * rows * inner + owner * tile, tile)
                out_ref[owner, part, array] = wide_out[array, pl.ds(start, tile), :].astype(BF16)
        return carry

    lax.fori_loop(0, owners, narrow, 0, unroll=2)


def attend(arrived, parts, together=4):
    sources, arrays, row, columns, feature = arrived.shape
    rows = sources * row
    return pl.pallas_call(
        lambda *refs: attend_kernel(together, *refs),
        out_shape=jax.ShapeDtypeStruct(
            (sources, parts, arrays, row * columns // parts, feature), BF16
        ),
        in_specs=[WHOLE],
        out_specs=WHOLE,
        scratch_shapes=[pltpu.VMEM((arrays, rows * columns, feature), F32)] * 2,
        compiler_params=pltpu.CompilerParams(vmem_limit_bytes=LIMIT),
        cost_estimate=pl.CostEstimate(
            flops=12 * columns * rows * rows * feature,
            bytes_accessed=4 * arrived.size,
            transcendentals=columns * rows * rows,
        ),
        name="attend",
    )(arrived)


def unpack_kernel(rows, in_ref, *refs):
    *out_refs, wide = refs
    sources, heads, arrays, tile, feature = in_ref.shape
    size = tile // rows * heads

    def step(source, carry):
        for array in range(arrays):
            base = array * tile * heads
            for head in range(heads):
                block = in_ref[source, head, array].astype(F32)
                wide[pl.ds(base + head, tile, stride=heads), :] = block
            for row in range(rows):
                to = pl.multiple_of(source * size, size)
                block = wide[pl.ds(base + row * size, size), :].astype(BF16)
                out_refs[array][row, pl.ds(to, size), :] = block
        return carry

    lax.fori_loop(0, sources, step, 0)


def unpack(returned, rows, steps=4):
    sources, heads, arrays, tile, feature = returned.shape
    width = sources * tile // rows * heads
    return pl.pallas_call(
        lambda *refs: unpack_kernel(rows, *refs),
        out_shape=[jax.ShapeDtypeStruct((rows, width, feature), BF16)] * arrays,
        grid=(steps,),
        in_specs=[
            pl.BlockSpec((sources // steps, heads, arrays, tile, feature), lambda i: (i, 0, 0, 0, 0))
        ],
        out_specs=[pl.BlockSpec((rows, width // steps, feature), lambda i: (0, i, 0))] * arrays,
        scratch_shapes=[pltpu.VMEM((arrays * tile * heads, feature), F32)],
        compiler_params=pltpu.CompilerParams(vmem_limit_bytes=LIMIT),
        name="unpack",
    )(returned)


def shards(*arrays):
    row_devs = lax.axis_size("row")
    head_devs = lax.axis_size("head")
    rows, columns, _, features = arrays[0].shape
    inner = columns // (row_devs * head_devs)
    count = len(arrays)

    packed = pack([a.reshape(rows, head_devs, row_devs, inner, features) for a in arrays])
    packed = packed.reshape(row_devs, count, rows, head_devs * inner, features)
    arrived = lax.all_to_all(packed, "row", 0, 0, tiled=True)
    results = attend(arrived, head_devs)
    results = results.reshape(row_devs * head_devs, count, rows * inner, features)
    returned = lax.all_to_all(results, NAMES, 0, 0, tiled=True)
    returned = returned.reshape(row_devs, head_devs, count, rows * inner, features)
    outs = unpack(returned, rows)
    return tuple(out.reshape(rows, columns // head_devs, head_devs, features) for out in outs)


def solution(mesh):
    spec_in = P("row", None, "head", None)
    spec_out = P("row", "head", None, None)
    return jax.shard_map(
        shards, mesh=mesh, in_specs=(spec_in,) * 4, out_specs=(spec_out,) * 4, check_vma=False
    )
```

```python
import functools

import jax
import jax.numpy as jnp
from jax import lax
from jax.experimental import pallas as pl
from jax.experimental.pallas import tpu as pltpu
from jax.sharding import Mesh, PartitionSpec as P

FINE = ("y", "z1", "z0", "x", "w", "core")
SIZES = (4, 2, 2, 4, 2, 2)
NEAR = ("y", "x", "core")
LAST = (((1,), (1,)), ((), ()))
FIRST = (((0,), (0,)), ((), ()))
F32 = jnp.float32
BF16 = jnp.bfloat16
LIMIT = 24 * 2**20
ALL = 58 * 2**20
LOG2E = 1.4426950408889634
ANY = pl.BlockSpec(memory_space=pl.ANY)
FAR = pl.BlockSpec(memory_space=pltpu.HBM)
WHOLE = pl.BlockSpec(memory_space=pltpu.VMEM)
SCALARS = pl.BlockSpec(memory_space=pltpu.SMEM)
ZS = 4


def other_run(w, chunk, z):
    return (w + chunk + jnp.where((z == 0) | (z == ZS - 1), 1, 0)) % 2


def dot(a, b, dims):
    return lax.dot_general(a, b, dims, preferred_element_type=F32)


def attend_column(query, key, value, cotangent):
    half = query.shape[0] // 2
    scale = query.shape[-1] ** (-0.5)
    causal = lax.broadcasted_iota(jnp.int32, (half, half), 0) <= lax.broadcasted_iota(
        jnp.int32, (half, half), 1
    )
    lows, grads = [], []
    for at in range(2):
        mine, keys = slice(at * half, (at + 1) * half), slice(0, (at + 1) * half)
        scores = dot(key[keys], query[mine], LAST) * (scale * LOG2E)
        grad_weights = dot(value[keys], cotangent[mine], LAST)
        diagonal = jnp.where(causal, scores[mine], -jnp.inf)
        scores = jnp.concatenate([scores[:half], diagonal], 0) if at else diagonal
        raw = jnp.exp2(scores - jnp.max(scores, axis=0, keepdims=True))
        weights = raw * (1.0 / jnp.sum(raw, axis=0, keepdims=True))
        dots = jnp.sum(weights * grad_weights, axis=0, keepdims=True)
        lows.append(weights.astype(BF16))
        grads.append(((grad_weights - dots) * (weights * scale)).astype(BF16))

    def to_queries(parts, other):
        return jnp.concatenate(
            [dot(parts[0], other[:half], FIRST), dot(parts[1], other, FIRST)], axis=0
        )

    def to_keys(parts, other):
        upper = jnp.concatenate([parts[0], jnp.zeros((half, half), BF16)], axis=0)
        both = jnp.concatenate([upper, parts[1]], axis=1)
        return jnp.dot(both, other, preferred_element_type=F32)

    return (
        to_queries(lows, value),
        to_queries(grads, key),
        to_keys(grads, query),
        to_keys(lows, cotangent),
    )


def pack_kernel(sizes, chunk, split, place_ref, *refs):
    ys, _, z0s, xs, _, cores = sizes
    *refs, held, sems = refs
    far_refs, out_refs = refs[:4], refs[4 + (not split) :]
    rows = far_refs[0].shape[0]
    my_z, my_w = place_ref[0] * z0s + place_ref[1], place_ref[2]
    copies = []
    for shift in range(ZS):
        z = (my_z + shift) % ZS
        quarter = other_run(my_w, chunk, z) * cores
        for array, ref in enumerate(far_refs):
            copy = pltpu.make_async_copy(
                ref.at[:, pl.ds(quarter, cores), :, z],
                held.at[shift, array],
                sems.at[shift, array],
            )
            copy.start()
            copies.append(copy)
    for shift in range(ZS):
        for copy in copies[shift * 4 : shift * 4 + 4]:
            copy.wait()

        def step(y, carry, shift=shift):
            for x in range(xs):
                for core in range(cores):
                    for array in range(4):
                        for row in range(rows):
                            tile = held[shift, array, row, core, y, x]
                            to = (y * xs + x) * cores + core
                            if split:
                                out_refs[shift][to, array, row] = tile
                            else:
                                out_refs[0][to, shift, array, row] = tile
            return carry

        lax.fori_loop(0, ys, step, 0)


def pack(arrays, place, sizes, chunk, split, after=()):
    ys, _, _, xs, _, cores = sizes
    rows, _, _, _, _, inner, feature = arrays[0].shape
    first, tail = ys * xs * cores, (len(arrays), rows, inner, feature)
    if split:
        shapes = [jax.ShapeDtypeStruct((first, *tail), BF16)] * ZS
    else:
        shapes = [jax.ShapeDtypeStruct((first, ZS, *tail), BF16)]
    return pl.pallas_call(
        lambda *refs: pack_kernel(sizes, chunk, split, *refs),
        out_shape=shapes,
        in_specs=[SCALARS] + [FAR] * 4 + [ANY] * len(after),
        out_specs=[WHOLE] * len(shapes),
        scratch_shapes=[
            pltpu.VMEM((ZS, 4, rows, cores, ys, xs, inner, feature), BF16),
            pltpu.SemaphoreType.DMA((ZS, 4)),
        ],
        compiler_params=pltpu.CompilerParams(vmem_limit_bytes=ALL),
        name="pack",
    )(place, *arrays, *after)


def attend_kernel(sizes, pieces, split, place_ref, *refs):
    ys, _, z0s, xs, _, cores = sizes
    in_refs, refs = refs[:pieces], refs[pieces + 1 :]
    *out_refs, wide_in, wide_out = refs
    sources = in_refs[0].shape[0]
    arrays, tile, feature = in_refs[0].shape[-3:]
    inner = tile // 4
    rows = ys * ZS * xs * 4
    my_z = place_ref[0] * z0s + place_ref[1]

    for shift in range(ZS):
        z = (my_z - shift + ZS) % ZS

        def widen(at, carry, shift=shift, z=z):
            y, x = at // xs, at % xs
            start = ((y * ZS + z) * xs + x) * tile
            for core in range(cores):
                for array in range(arrays):
                    source = at * cores + core
                    if pieces == 1:
                        block = in_refs[0][source, shift, array]
                    else:
                        block = in_refs[shift][source, array]
                    to = pl.multiple_of(core * rows * inner + start, tile)
                    wide_in[array, pl.ds(to, tile), :] = block.astype(F32)
            return carry

        lax.fori_loop(0, sources // cores, widen, 0, unroll=2)

    def column(core, carry):
        for place in range(inner):
            spot = pl.ds(core * rows * inner + place, rows, stride=inner)
            block = [wide_in[array, spot, :].astype(BF16) for array in range(arrays)]
            for array, result in enumerate(attend_column(*block)):
                wide_out[array, spot, :] = result
        return carry

    lax.fori_loop(0, cores, column, 0)

    for shift in range(ZS):
        z = my_z ^ shift

        def narrow(at, carry, shift=shift, z=z):
            y, x = at // xs, at % xs
            start = ((y * ZS + z) * xs + x) * tile
            for array in range(arrays):
                for core in range(cores):
                    spot = pl.ds(pl.multiple_of(core * rows * inner + start, tile), tile)
                    block = wide_out[array, spot, :].astype(BF16)
                    to = slice(core * tile, (core + 1) * tile)
                    if split:
                        out_refs[shift][at, array, to] = block
                    else:
                        out_refs[0][at, shift, array, to] = block
            return carry

        lax.fori_loop(0, ys * xs, narrow, 0, unroll=2)


def attend(pieces, place, sizes, split, after):
    ys, _, _, xs, _, cores = sizes
    arrays, tile, feature = pieces[0].shape[-3:]
    rows = ys * ZS * xs * 4
    columns = tile // 4 * cores
    tail = (arrays, tile * cores, feature)
    if split:
        shapes = [jax.ShapeDtypeStruct((ys * xs, *tail), BF16)] * ZS
    else:
        shapes = [jax.ShapeDtypeStruct((ys * xs, ZS, *tail), BF16)]
    return pl.pallas_call(
        lambda *refs: attend_kernel(sizes, len(pieces), split, *refs),
        out_shape=shapes,
        in_specs=[SCALARS] + [WHOLE] * len(pieces) + [ANY],
        out_specs=[WHOLE] * len(shapes),
        scratch_shapes=[pltpu.VMEM((arrays, rows * columns, feature), F32)] * 2,
        compiler_params=pltpu.CompilerParams(vmem_limit_bytes=LIMIT),
        cost_estimate=pl.CostEstimate(flops=0, bytes_accessed=0, transcendentals=0),
        name="attend",
    )(place, *pieces, after)


def join_kernel(*refs):
    *in_refs, _, out_ref = refs
    for side, ref in enumerate(in_refs):
        out_ref[:, side] = ref[...]


def join(pieces, after):
    first, *tail = pieces[0].shape
    return pl.pallas_call(
        join_kernel,
        out_shape=jax.ShapeDtypeStruct((first, len(pieces), *tail), BF16),
        in_specs=[WHOLE] * len(pieces) + [ANY],
        out_specs=WHOLE,
        compiler_params=pltpu.CompilerParams(vmem_limit_bytes=LIMIT),
        name="join",
    )(*pieces, after)


def part_kernel(in_ref, _, *refs):
    *out_refs, sems = refs
    copies = [
        pltpu.make_async_copy(in_ref.at[:, shift], ref, sems.at[shift])
        for shift, ref in enumerate(out_refs)
    ]
    for copy in copies:
        copy.start()
    for copy in copies:
        copy.wait()


def part(joined, after):
    first, shifts, *tail = joined.shape
    return pl.pallas_call(
        part_kernel,
        out_shape=[jax.ShapeDtypeStruct((first, *tail), BF16)] * shifts,
        in_specs=[FAR, ANY],
        out_specs=[WHOLE] * shifts,
        scratch_shapes=[pltpu.SemaphoreType.DMA((shifts,))],
        compiler_params=pltpu.CompilerParams(vmem_limit_bytes=ALL),
        name="part",
    )(joined, after)


def hold_kernel(*refs):
    refs[-1][...] = jnp.zeros_like(refs[-1])


def hold(waited, flops=10**12):
    return pl.pallas_call(
        hold_kernel,
        out_shape=jax.ShapeDtypeStruct((8, 128), F32),
        in_specs=[ANY] * len(waited),
        out_specs=WHOLE,
        cost_estimate=pl.CostEstimate(flops=flops, bytes_accessed=4096, transcendentals=0),
        name="hold",
    )(*waited)


def unpack_kernel(sizes, place_ref, _, first_ref, *refs):
    _, _, z0s, xs, ws, cores = sizes
    second_refs, refs = refs[:ZS], refs[ZS:]
    *out_refs, wide = refs
    arrays, tile, feature = first_ref.shape[-3:]
    rows = out_refs[0].shape[0]
    heads = ws * cores
    some = tile // cores
    size = some // rows * heads
    my_z, my_w = place_ref[0] * z0s + place_ref[1], place_ref[2]
    for shift in range(ZS):
        z = my_z ^ shift
        run = other_run(my_w, 0, z)

        def step(x, carry, shift=shift, z=z, runs=(0, 1)):
            for array in range(arrays):
                base = array * some * heads
                for chunk in range(2):
                    ref = first_ref if chunk == 0 else second_refs[shift]
                    block = (ref[x, shift, array] if chunk == 0 else ref[x, array]).astype(F32)
                    for core in range(cores):
                        spot = pl.ds(base + runs[chunk] * cores + core, some, stride=heads)
                        wide[spot, :] = block[core * some : (core + 1) * some]
                for row in range(rows):
                    to = pl.multiple_of((z * xs + x) * size, size)
                    block = wide[pl.ds(base + row * size, size), :].astype(BF16)
                    out_refs[array][row, pl.ds(to, size), :] = block
            return carry

        for which in range(ws):

            @pl.when(run == which)
            def _(step=step, which=which):
                lax.fori_loop(0, xs, functools.partial(step, runs=(which, 1 - which)), 0)


def unpack(first, second, place, sizes, rows, after):
    ys, _, _, xs, ws, cores = sizes
    arrays, tile, feature = first.shape[-3:]
    width = ys * ZS * xs * tile // rows * ws
    return pl.pallas_call(
        lambda *refs: unpack_kernel(sizes, *refs),
        out_shape=[jax.ShapeDtypeStruct((rows, width, feature), BF16)] * arrays,
        grid=(ys,),
        in_specs=[SCALARS, ANY]
        + [pl.BlockSpec((xs, ZS, arrays, tile, feature), lambda i: (i, 0, 0, 0, 0))]
        + [pl.BlockSpec((xs, arrays, tile, feature), lambda i: (i, 0, 0, 0))] * ZS,
        out_specs=[pl.BlockSpec((rows, width // ys, feature), lambda i: (0, i, 0))] * arrays,
        scratch_shapes=[pltpu.VMEM((arrays * tile * ws, feature), F32)],
        compiler_params=pltpu.CompilerParams(vmem_limit_bytes=ALL),
        name="unpack",
    )(place, after, first, *second)


def z_in(pieces):
    return [pieces[0]] + [
        lax.ppermute(
            pieces[k], ("z1", "z0"), [(z, (z + k) % ZS) for z in range(ZS)]
        )
        for k in range(1, ZS)
    ]


def z_out(pieces, chunk):
    def pairs(shift):
        made = []
        for z in range(ZS):
            for w in range(2):
                to = (w + chunk + (z in (0, ZS - 1))) % 2
                made.append((z * 2 + w, (z ^ shift) * 2 + to))
        return made

    return [lax.ppermute(pieces[k], ("z1", "z0", "w"), pairs(k)) for k in range(ZS)]


def shards(*arrays):
    sizes = tuple(lax.axis_size(name) for name in FINE)
    ys, z1s, z0s, xs, ws, cores = sizes
    rows, columns, _, feature = arrays[0].shape
    owners = ys * z1s * z0s * xs
    inner = columns // (owners * ws * cores)
    arrays = [a.reshape(rows, ws * cores, ys, ZS, xs, inner, feature) for a in arrays]
    place = jnp.stack([lax.axis_index(name) for name in ("z1", "z0", "w")]).astype(jnp.int32)

    def flat(piece):
        return piece.reshape(*piece.shape[:-3], rows * inner, feature)

    def across(whole, names):
        return lax.all_to_all(whole, names, 0, 0, tiled=True)

    packed = [flat(p) for p in pack(arrays, place, sizes, 0, True)]
    second = flat(pack(arrays, place, sizes, 1, False, packed[:1])[0])
    first = z_in(packed)
    pieces = part(across(second, NEAR), hold(first[1:]))
    second = z_in(pieces)
    first = across(join(first, pieces[0]), NEAR)

    done = attend([first], place, sizes, True, hold(second[2:3]))
    first = z_out(done, 0)
    second = attend(second, place, sizes, False, done[0])[0]
    pieces = part(across(second, ("y", "x")), hold(first))
    second = z_out(pieces, 1)
    first = across(join(first, pieces[0]), ("y", "x"))

    results = unpack(first, second, place, sizes, rows, hold(second))
    return tuple(r.reshape(rows, columns // (ws * cores), ws * cores, feature) for r in results)


def solution(mesh):
    fine = Mesh(mesh.devices.reshape(SIZES), FINE)
    row, head = FINE[:4], FINE[4:]
    spec_in = P(row, None, head, None)
    spec_out = P(row, head, None, None)
    return jax.shard_map(
        shards, mesh=fine, in_specs=(spec_in,) * 4, out_specs=(spec_out,) * 4, check_vma=False
    )
```

```python
import functools

import jax
import jax.numpy as jnp
from jax import lax
from jax.experimental import pallas as pl
from jax.experimental.pallas import tpu as pltpu
from jax.sharding import Mesh, PartitionSpec as P

FINE = ("y", "z1", "z0", "x", "w", "core")
SIZES = (4, 2, 2, 4, 2, 2)
NEAR = ("y", "x", "core")
LAST = (((1,), (1,)), ((), ()))
FIRST = (((0,), (0,)), ((), ()))
F32 = jnp.float32
BF16 = jnp.bfloat16
LIMIT = 24 * 2**20
ALL = 58 * 2**20
LOG2E = 1.4426950408889634
ANY = pl.BlockSpec(memory_space=pl.ANY)
FAR = pl.BlockSpec(memory_space=pltpu.HBM)
WHOLE = pl.BlockSpec(memory_space=pltpu.VMEM)
SCALARS = pl.BlockSpec(memory_space=pltpu.SMEM)
ZS = 4


def other_run(w, z):
    return (w + jnp.where((z == 0) | (z == ZS - 1), 1, 0)) % 2


def dot(a, b, dims):
    return lax.dot_general(a, b, dims, preferred_element_type=F32)


def attend_column(query, key, value, cotangent):
    half = query.shape[0] // 2
    scale = query.shape[-1] ** (-0.5)
    causal = lax.broadcasted_iota(jnp.int32, (half, half), 0) <= lax.broadcasted_iota(
        jnp.int32, (half, half), 1
    )
    lows, grads = [], []
    for at in range(2):
        mine, keys = slice(at * half, (at + 1) * half), slice(0, (at + 1) * half)
        scores = dot(key[keys], query[mine], LAST) * (scale * LOG2E)
        grad_weights = dot(value[keys], cotangent[mine], LAST)
        diagonal = jnp.where(causal, scores[mine], -jnp.inf)
        scores = jnp.concatenate([scores[:half], diagonal], 0) if at else diagonal
        raw = jnp.exp2(scores - jnp.max(scores, axis=0, keepdims=True))
        weights = raw * (1.0 / jnp.sum(raw, axis=0, keepdims=True))
        dots = jnp.sum(weights * grad_weights, axis=0, keepdims=True)
        lows.append(weights.astype(BF16))
        grads.append(((grad_weights - dots) * (weights * scale)).astype(BF16))

    def to_queries(parts, other):
        return jnp.concatenate(
            [dot(parts[0], other[:half], FIRST), dot(parts[1], other, FIRST)], axis=0
        )

    def to_keys(parts, other):
        upper = jnp.concatenate([parts[0], jnp.zeros((half, half), BF16)], axis=0)
        both = jnp.concatenate([upper, parts[1]], axis=1)
        return jnp.dot(both, other, preferred_element_type=F32)

    return (
        to_queries(lows, value),
        to_queries(grads, key),
        to_keys(grads, query),
        to_keys(lows, cotangent),
    )


def pack_kernel(sizes, chunk, split, place_ref, *refs):
    ys, _, z0s, xs, _, cores = sizes
    *refs, held, sems = refs
    far_refs, out_refs = refs[:4], refs[4 + (not split) :]
    rows = far_refs[0].shape[0]
    my_z, my_w = place_ref[0] * z0s + place_ref[1], place_ref[2]
    copies = []
    for shift in range(ZS):
        z = (my_z + shift) % ZS
        quarter, slot = other_run(my_w, z) * cores, z // 2 * 2 + chunk
        for array, ref in enumerate(far_refs):
            copy = pltpu.make_async_copy(
                ref.at[:, pl.ds(quarter, cores), :, slot],
                held.at[shift, array],
                sems.at[shift, array],
            )
            copy.start()
            copies.append(copy)
    for shift in range(ZS):
        for copy in copies[shift * 4 : shift * 4 + 4]:
            copy.wait()

        def step(y, carry, shift=shift):
            for x in range(xs):
                for core in range(cores):
                    for array in range(4):
                        for row in range(rows):
                            tile = held[shift, array, row, core, y, x]
                            to = (y * xs + x) * cores + core
                            if split:
                                out_refs[shift][to, array, row] = tile
                            else:
                                out_refs[0][to, shift, array, row] = tile
            return carry

        lax.fori_loop(0, ys, step, 0)


def pack(arrays, place, sizes, chunk, split, after=()):
    ys, _, _, xs, _, cores = sizes
    rows, _, _, _, _, inner, feature = arrays[0].shape
    first, tail = ys * xs * cores, (len(arrays), rows, inner, feature)
    if split:
        shapes = [jax.ShapeDtypeStruct((first, *tail), BF16)] * ZS
    else:
        shapes = [jax.ShapeDtypeStruct((first, ZS, *tail), BF16)]
    return pl.pallas_call(
        lambda *refs: pack_kernel(sizes, chunk, split, *refs),
        out_shape=shapes,
        in_specs=[SCALARS] + [FAR] * 4 + [ANY] * len(after),
        out_specs=[WHOLE] * len(shapes),
        scratch_shapes=[
            pltpu.VMEM((ZS, 4, rows, cores, ys, xs, inner, feature), BF16),
            pltpu.SemaphoreType.DMA((ZS, 4)),
        ],
        compiler_params=pltpu.CompilerParams(vmem_limit_bytes=ALL),
        name="pack",
    )(place, *arrays, *after)


def attend_kernel(sizes, pieces, split, place_ref, *refs):
    ys, _, z0s, xs, _, cores = sizes
    in_refs, refs = refs[:pieces], refs[pieces + 1 :]
    *out_refs, wide_in, wide_out = refs
    sources = in_refs[0].shape[0]
    arrays, tile, feature = in_refs[0].shape[-3:]
    inner = tile // 4
    rows = ys * ZS * xs * 4
    my_z = place_ref[0] * z0s + place_ref[1]

    for shift in range(ZS):
        z = (my_z - shift + ZS) % ZS

        def widen(at, carry, shift=shift, z=z):
            y, x = at // xs, at % xs
            start = ((y * ZS + z) * xs + x) * tile
            for core in range(cores):
                for array in range(arrays):
                    source = at * cores + core
                    if pieces == 1:
                        block = in_refs[0][source, shift, array]
                    else:
                        block = in_refs[shift][source, array]
                    to = pl.multiple_of(core * rows * inner + start, tile)
                    wide_in[array, pl.ds(to, tile), :] = block.astype(F32)
            return carry

        lax.fori_loop(0, sources // cores, widen, 0, unroll=2)

    def column(core, carry):
        for place in range(inner):
            spot = pl.ds(core * rows * inner + place, rows, stride=inner)
            block = [wide_in[array, spot, :].astype(BF16) for array in range(arrays)]
            for array, result in enumerate(attend_column(*block)):
                wide_out[array, spot, :] = result
        return carry

    lax.fori_loop(0, cores, column, 0)

    for shift in range(ZS):
        z = my_z ^ shift

        def narrow(at, carry, shift=shift, z=z):
            y, x = at // xs, at % xs
            start = ((y * ZS + z) * xs + x) * tile
            for array in range(arrays):
                for core in range(cores):
                    spot = pl.ds(pl.multiple_of(core * rows * inner + start, tile), tile)
                    block = wide_out[array, spot, :].astype(BF16)
                    to = slice(core * tile, (core + 1) * tile)
                    if split:
                        out_refs[shift][at, array, to] = block
                    else:
                        out_refs[0][at, shift, array, to] = block
            return carry

        lax.fori_loop(0, ys * xs, narrow, 0, unroll=2)


def attend(pieces, place, sizes, split, after):
    ys, _, _, xs, _, cores = sizes
    arrays, tile, feature = pieces[0].shape[-3:]
    rows = ys * ZS * xs * 4
    columns = tile // 4 * cores
    tail = (arrays, tile * cores, feature)
    if split:
        shapes = [jax.ShapeDtypeStruct((ys * xs, *tail), BF16)] * ZS
    else:
        shapes = [jax.ShapeDtypeStruct((ys * xs, ZS, *tail), BF16)]
    return pl.pallas_call(
        lambda *refs: attend_kernel(sizes, len(pieces), split, *refs),
        out_shape=shapes,
        in_specs=[SCALARS] + [WHOLE] * len(pieces) + [ANY],
        out_specs=[WHOLE] * len(shapes),
        scratch_shapes=[pltpu.VMEM((arrays, rows * columns, feature), F32)] * 2,
        compiler_params=pltpu.CompilerParams(vmem_limit_bytes=LIMIT),
        cost_estimate=pl.CostEstimate(flops=0, bytes_accessed=0, transcendentals=0),
        name="attend",
    )(place, *pieces, after)


def join_kernel(*refs):
    *in_refs, _, out_ref = refs
    for side, ref in enumerate(in_refs):
        out_ref[:, side] = ref[...]


def join(pieces, after):
    first, *tail = pieces[0].shape
    return pl.pallas_call(
        join_kernel,
        out_shape=jax.ShapeDtypeStruct((first, len(pieces), *tail), BF16),
        in_specs=[WHOLE] * len(pieces) + [ANY],
        out_specs=WHOLE,
        compiler_params=pltpu.CompilerParams(vmem_limit_bytes=LIMIT),
        name="join",
    )(*pieces, after)


def part_kernel(in_ref, _, *refs):
    *out_refs, sems = refs
    copies = [
        pltpu.make_async_copy(in_ref.at[:, shift], ref, sems.at[shift])
        for shift, ref in enumerate(out_refs)
    ]
    for copy in copies:
        copy.start()
    for copy in copies:
        copy.wait()


def part(joined, after):
    first, shifts, *tail = joined.shape
    return pl.pallas_call(
        part_kernel,
        out_shape=[jax.ShapeDtypeStruct((first, *tail), BF16)] * shifts,
        in_specs=[FAR, ANY],
        out_specs=[WHOLE] * shifts,
        scratch_shapes=[pltpu.SemaphoreType.DMA((shifts,))],
        compiler_params=pltpu.CompilerParams(vmem_limit_bytes=ALL),
        name="part",
    )(joined, after)


def hold_kernel(*refs):
    refs[-1][...] = jnp.zeros_like(refs[-1])


def hold(waited, flops=10**12):
    return pl.pallas_call(
        hold_kernel,
        out_shape=jax.ShapeDtypeStruct((8, 128), F32),
        in_specs=[ANY] * len(waited),
        out_specs=WHOLE,
        cost_estimate=pl.CostEstimate(flops=flops, bytes_accessed=4096, transcendentals=0),
        name="hold",
    )(*waited)


def unpack_kernel(sizes, place_ref, _, first_ref, *refs):
    _, _, z0s, xs, ws, cores = sizes
    second_refs, refs = refs[:ZS], refs[ZS:]
    *out_refs, wide = refs
    arrays, tile, feature = first_ref.shape[-3:]
    rows = out_refs[0].shape[0]
    heads = ws * cores
    some = tile // cores
    size = some // rows * heads
    my_z, my_w = place_ref[0] * z0s + place_ref[1], place_ref[2]
    for pair in range(ZS // 2):
        z = my_z ^ (2 * pair)
        run = other_run(my_w, z)

        def step(x, carry, pair=pair, z=z, runs=(0, 1)):
            for chunk in range(2):
                slot = z // 2 * 2 + chunk
                for array in range(arrays):
                    base = (chunk * arrays + array) * some * heads
                    for side in range(2):
                        at = 2 * pair + side
                        block = first_ref[x, at, array] if chunk == 0 else second_refs[at][x, array]
                        block = block.astype(F32)
                        for core in range(cores):
                            spot = pl.ds(base + runs[side] * cores + core, some, stride=heads)
                            wide[spot, :] = block[core * some : (core + 1) * some]
                    for row in range(rows):
                        to = pl.multiple_of((slot * xs + x) * size, size)
                        block = wide[pl.ds(base + row * size, size), :].astype(BF16)
                        out_refs[array][row, pl.ds(to, size), :] = block
            return carry

        for which in range(ws):

            @pl.when(run == which)
            def _(step=step, which=which):
                lax.fori_loop(0, xs, functools.partial(step, runs=(which, 1 - which)), 0)


def unpack(first, second, place, sizes, rows, after):
    ys, _, _, xs, ws, cores = sizes
    arrays, tile, feature = first.shape[-3:]
    width = ys * ZS * xs * tile // rows * ws
    return pl.pallas_call(
        lambda *refs: unpack_kernel(sizes, *refs),
        out_shape=[jax.ShapeDtypeStruct((rows, width, feature), BF16)] * arrays,
        grid=(ys,),
        in_specs=[SCALARS, ANY]
        + [pl.BlockSpec((xs, ZS, arrays, tile, feature), lambda i: (i, 0, 0, 0, 0))]
        + [pl.BlockSpec((xs, arrays, tile, feature), lambda i: (i, 0, 0, 0))] * ZS,
        out_specs=[pl.BlockSpec((rows, width // ys, feature), lambda i: (0, i, 0))] * arrays,
        scratch_shapes=[pltpu.VMEM((2 * arrays * tile * ws, feature), F32)],
        compiler_params=pltpu.CompilerParams(vmem_limit_bytes=ALL),
        name="unpack",
    )(place, after, first, *second)


def z_in(pieces):
    return [pieces[0]] + [
        lax.ppermute(
            pieces[k], ("z1", "z0"), [(z, (z + k) % ZS) for z in range(ZS)]
        )
        for k in range(1, ZS)
    ]


def z_out(pieces):
    def pairs(shift):
        made = []
        for z in range(ZS):
            for w in range(2):
                to = (w + (z in (0, ZS - 1))) % 2
                made.append((z * 2 + w, (z ^ shift) * 2 + to))
        return made

    return [lax.ppermute(pieces[k], ("z1", "z0", "w"), pairs(k)) for k in range(ZS)]


def shards(*arrays):
    sizes = tuple(lax.axis_size(name) for name in FINE)
    ys, z1s, z0s, xs, ws, cores = sizes
    rows, columns, _, feature = arrays[0].shape
    owners = ys * z1s * z0s * xs
    inner = columns // (owners * ws * cores)
    arrays = [a.reshape(rows, ws * cores, ys, ZS, xs, inner, feature) for a in arrays]
    place = jnp.stack([lax.axis_index(name) for name in ("z1", "z0", "w")]).astype(jnp.int32)

    def flat(piece):
        return piece.reshape(*piece.shape[:-3], rows * inner, feature)

    def across(whole, names):
        return lax.all_to_all(whole, names, 0, 0, tiled=True)

    packed = [flat(p) for p in pack(arrays, place, sizes, 0, True)]
    second = flat(pack(arrays, place, sizes, 1, False, packed[:1])[0])
    first = z_in(packed)
    pieces = part(across(second, NEAR), hold(first[1:]))
    second = z_in(pieces)
    first = across(join(first, pieces[0]), NEAR)

    done = attend([first], place, sizes, True, hold(second[2:3]))
    first = z_out(done)
    second = attend(second, place, sizes, False, done[0])[0]
    pieces = part(across(second, ("y", "x")), hold(first))
    second = z_out(pieces)
    first = across(join(first, pieces[0]), ("y", "x"))

    results = unpack(first, second, place, sizes, rows, hold(second))
    return tuple(r.reshape(rows, columns // (ws * cores), ws * cores, feature) for r in results)


def solution(mesh):
    fine = Mesh(mesh.devices.reshape(SIZES), FINE)
    row, head = FINE[:4], FINE[4:]
    spec_in = P(row, None, head, None)
    spec_out = P(row, head, None, None)
    return jax.shard_map(
        shards, mesh=fine, in_specs=(spec_in,) * 4, out_specs=(spec_out,) * 4, check_vma=False
    )
```

```python
import functools

import jax
import jax.numpy as jnp
from jax import lax
from jax.experimental import pallas as pl
from jax.experimental.pallas import tpu as pltpu
from jax.sharding import Mesh, PartitionSpec as P

FINE = ("y", "z1", "z0", "x", "w", "core")
SIZES = (4, 2, 2, 4, 2, 2)
NEAR = ("y", "x", "core")
LAST = (((1,), (1,)), ((), ()))
FIRST = (((0,), (0,)), ((), ()))
F32 = jnp.float32
BF16 = jnp.bfloat16
LIMIT = 24 * 2**20
SMALL = 6 * 2**20
ALL = 58 * 2**20
LOG2E = 1.4426950408889634
ANY = pl.BlockSpec(memory_space=pl.ANY)
FAR = pl.BlockSpec(memory_space=pltpu.HBM)
WHOLE = pl.BlockSpec(memory_space=pltpu.VMEM)
SCALARS = pl.BlockSpec(memory_space=pltpu.SMEM)
ZS = 4


def other_run(w, z):
    return (w + jnp.where((z == 0) | (z == ZS - 1), 1, 0)) % 2


def dot(a, b, dims):
    return lax.dot_general(a, b, dims, preferred_element_type=F32)


def attend_column(query, key, value, cotangent):
    half = query.shape[0] // 2
    scale = query.shape[-1] ** (-0.5)
    causal = lax.broadcasted_iota(jnp.int32, (half, half), 0) <= lax.broadcasted_iota(
        jnp.int32, (half, half), 1
    )
    lows, grads = [], []
    for at in range(2):
        mine, keys = slice(at * half, (at + 1) * half), slice(0, (at + 1) * half)
        scores = dot(key[keys], query[mine], LAST) * (scale * LOG2E)
        grad_weights = dot(value[keys], cotangent[mine], LAST)
        diagonal = jnp.where(causal, scores[mine], -jnp.inf)
        scores = jnp.concatenate([scores[:half], diagonal], 0) if at else diagonal
        raw = jnp.exp2(scores - jnp.max(scores, axis=0, keepdims=True))
        weights = raw * (1.0 / jnp.sum(raw, axis=0, keepdims=True))
        dots = jnp.sum(weights * grad_weights, axis=0, keepdims=True)
        lows.append(weights.astype(BF16))
        grads.append(((grad_weights - dots) * (weights * scale)).astype(BF16))

    def to_queries(parts, other):
        return jnp.concatenate(
            [dot(parts[0], other[:half], FIRST), dot(parts[1], other, FIRST)], axis=0
        )

    def to_keys(parts, other):
        upper = jnp.concatenate([parts[0], jnp.zeros((half, half), BF16)], axis=0)
        both = jnp.concatenate([upper, parts[1]], axis=1)
        return jnp.dot(both, other, preferred_element_type=F32)

    return (
        to_queries(lows, value),
        to_queries(grads, key),
        to_keys(grads, query),
        to_keys(lows, cotangent),
    )


def sending(made, out_refs, split, shift, sems):
    to = out_refs[shift] if split else out_refs[0].at[:, shift]
    copy = pltpu.make_async_copy(made.at[shift], to, sems.at[shift])
    copy.start()
    return copy


def pack_kernel(sizes, chunk, split, place_ref, *refs):
    ys, _, z0s, xs, _, cores = sizes
    *refs, held, made, sems, out_sems = refs
    far_refs, out_refs = refs[:4], refs[4 + (not split) :]
    rows = far_refs[0].shape[0]
    my_z, my_w = place_ref[0] * z0s + place_ref[1], place_ref[2]
    copies, sent = [], []
    for shift in range(ZS):
        z = (my_z + shift) % ZS
        quarter, slot = other_run(my_w, z) * cores, z // 2 * 2 + chunk
        for array, ref in enumerate(far_refs):
            copy = pltpu.make_async_copy(
                ref.at[:, pl.ds(quarter, cores), :, slot],
                held.at[shift, array],
                sems.at[shift, array],
            )
            copy.start()
            copies.append(copy)
    for shift in range(ZS):
        for copy in copies[shift * 4 : shift * 4 + 4]:
            copy.wait()

        def step(y, carry, shift=shift):
            for x in range(xs):
                for core in range(cores):
                    for array in range(4):
                        for row in range(rows):
                            to = (y * xs + x) * cores + core
                            made[shift, to, array, row] = held[shift, array, row, core, y, x]
            return carry

        lax.fori_loop(0, ys, step, 0)
        sent.append(sending(made, out_refs, split, shift, out_sems))
    for copy in sent:
        copy.wait()


def pack(arrays, place, sizes, chunk, split, after=()):
    ys, _, _, xs, _, cores = sizes
    rows, _, _, _, _, inner, feature = arrays[0].shape
    first, tail = ys * xs * cores, (len(arrays), rows, inner, feature)
    if split:
        shapes = [jax.ShapeDtypeStruct((first, *tail), BF16)] * ZS
    else:
        shapes = [jax.ShapeDtypeStruct((first, ZS, *tail), BF16)]
    return pl.pallas_call(
        lambda *refs: pack_kernel(sizes, chunk, split, *refs),
        out_shape=shapes,
        in_specs=[SCALARS] + [FAR] * 4 + [ANY] * len(after),
        out_specs=[FAR] * len(shapes),
        scratch_shapes=[
            pltpu.VMEM((ZS, 4, rows, cores, ys, xs, inner, feature), BF16),
            pltpu.VMEM((ZS, first, *tail), BF16),
            pltpu.SemaphoreType.DMA((ZS, 4)),
            pltpu.SemaphoreType.DMA((ZS,)),
        ],
        compiler_params=pltpu.CompilerParams(vmem_limit_bytes=ALL),
        name="pack",
    )(place, *arrays, *after)


def attend_kernel(sizes, pieces, split, place_ref, *refs):
    ys, _, z0s, xs, _, cores = sizes
    in_refs, refs = refs[:pieces], refs[pieces + 1 :]
    *out_refs, wide_in, wide_out, made, out_sems = refs
    sent = []
    sources = in_refs[0].shape[0]
    arrays, tile, feature = in_refs[0].shape[-3:]
    inner = tile // 4
    rows = ys * ZS * xs * 4
    my_z = place_ref[0] * z0s + place_ref[1]

    for shift in range(ZS):
        z = (my_z - shift + ZS) % ZS

        def widen(at, carry, shift=shift, z=z):
            y, x = at // xs, at % xs
            start = ((y * ZS + z) * xs + x) * tile
            for core in range(cores):
                for array in range(arrays):
                    source = at * cores + core
                    if pieces == 1:
                        block = in_refs[0][source, shift, array]
                    else:
                        block = in_refs[shift][source, array]
                    to = pl.multiple_of(core * rows * inner + start, tile)
                    wide_in[array, pl.ds(to, tile), :] = block.astype(F32)
            return carry

        lax.fori_loop(0, sources // cores, widen, 0, unroll=2)

    def column(core, carry):
        for place in range(inner):
            spot = pl.ds(core * rows * inner + place, rows, stride=inner)
            block = [wide_in[array, spot, :].astype(BF16) for array in range(arrays)]
            for array, result in enumerate(attend_column(*block)):
                wide_out[array, spot, :] = result
        return carry

    lax.fori_loop(0, cores, column, 0)

    for shift in range(ZS):
        z = my_z ^ shift

        def narrow(at, carry, shift=shift, z=z):
            y, x = at // xs, at % xs
            start = ((y * ZS + z) * xs + x) * tile
            for array in range(arrays):
                for core in range(cores):
                    spot = pl.ds(pl.multiple_of(core * rows * inner + start, tile), tile)
                    block = wide_out[array, spot, :].astype(BF16)
                    made[shift, at, array, core * tile : (core + 1) * tile] = block
            return carry

        lax.fori_loop(0, ys * xs, narrow, 0, unroll=2)
        sent.append(sending(made, out_refs, split, shift, out_sems))
    for copy in sent:
        copy.wait()


def attend(pieces, place, sizes, split, after):
    ys, _, _, xs, _, cores = sizes
    arrays, tile, feature = pieces[0].shape[-3:]
    rows = ys * ZS * xs * 4
    columns = tile // 4 * cores
    tail = (arrays, tile * cores, feature)
    if split:
        shapes = [jax.ShapeDtypeStruct((ys * xs, *tail), BF16)] * ZS
    else:
        shapes = [jax.ShapeDtypeStruct((ys * xs, ZS, *tail), BF16)]
    return pl.pallas_call(
        lambda *refs: attend_kernel(sizes, len(pieces), split, *refs),
        out_shape=shapes,
        in_specs=[SCALARS] + [WHOLE] * len(pieces) + [ANY],
        out_specs=[FAR] * len(shapes),
        scratch_shapes=[
            pltpu.VMEM((arrays, rows * columns, feature), F32),
            pltpu.VMEM((arrays, rows * columns, feature), F32),
            pltpu.VMEM((ZS, ys * xs, *tail), BF16),
            pltpu.SemaphoreType.DMA((ZS,)),
        ],
        compiler_params=pltpu.CompilerParams(vmem_limit_bytes=LIMIT),
        cost_estimate=pl.CostEstimate(flops=0, bytes_accessed=0, transcendentals=0),
        name="attend",
    )(place, *pieces, after)


def relay(sources, targets, held, sems):
    first = held.shape[1]
    cuts = [0, first // 2, first] if first > 1 else [0, first]
    steps = []
    for at, (source, target) in enumerate(zip(sources, targets)):
        for part_at in range(len(cuts) - 1):
            some = slice(cuts[part_at], cuts[part_at + 1])
            spot, sem = held.at[at, some], sems.at[at, part_at]
            into = pltpu.make_async_copy(source.at[some], spot, sem.at[0])
            out = pltpu.make_async_copy(spot, target.at[some], sem.at[1])
            into.start()
            steps.append((into, out))
    for into, out in steps:
        into.wait()
        out.start()
    for _, out in steps:
        out.wait()


def relay_scratch(count, shape):
    return [pltpu.VMEM((count, *shape), BF16), pltpu.SemaphoreType.DMA((count, 2, 2))]


def join_kernel(*refs):
    *in_refs, _, out_ref, held, sems = refs
    relay(in_refs, [out_ref.at[:, k] for k in range(len(in_refs))], held, sems)


def join(pieces, after):
    first, *tail = pieces[0].shape
    count = len(pieces)
    return pl.pallas_call(
        join_kernel,
        out_shape=jax.ShapeDtypeStruct((first, count, *tail), BF16),
        in_specs=[ANY] * (count + 1),
        out_specs=ANY,
        scratch_shapes=relay_scratch(count, (first, *tail)),
        compiler_params=pltpu.CompilerParams(vmem_limit_bytes=SMALL),
        name="join",
    )(*pieces, after)


def part_kernel(picks, in_ref, _, *refs):
    *out_refs, held, sems = refs
    relay([in_ref.at[:, pick] for pick in picks], out_refs, held, sems)


def part(joined, after, picks):
    first, _, *tail = joined.shape
    count = len(picks)
    return pl.pallas_call(
        lambda *refs: part_kernel(picks, *refs),
        out_shape=[jax.ShapeDtypeStruct((first, *tail), BF16)] * count,
        in_specs=[ANY] * 2,
        out_specs=[ANY] * count,
        scratch_shapes=relay_scratch(count, (first, *tail)),
        compiler_params=pltpu.CompilerParams(vmem_limit_bytes=SMALL),
        name="part",
    )(joined, after)


def parts(joined, after, early):
    late = [k for k in range(ZS) if k not in early]
    made = part(joined, after, early)
    found = dict(zip(early, made)) | dict(zip(late, part(joined, made[0], late)))
    return [found[k] for k in range(ZS)]


def hold_kernel(*refs):
    refs[-1][...] = jnp.zeros_like(refs[-1])


def hold(waited, flops=10**12):
    return pl.pallas_call(
        hold_kernel,
        out_shape=jax.ShapeDtypeStruct((8, 128), F32),
        in_specs=[ANY] * len(waited),
        out_specs=WHOLE,
        compiler_params=pltpu.CompilerParams(vmem_limit_bytes=SMALL),
        cost_estimate=pl.CostEstimate(flops=flops, bytes_accessed=4096, transcendentals=0),
        name="hold",
    )(*waited)


def unpack_kernel(sizes, place_ref, _, first_ref, *refs):
    _, _, z0s, xs, ws, cores = sizes
    second_refs, refs = refs[:ZS], refs[ZS:]
    *out_refs, wide = refs
    arrays, tile, feature = first_ref.shape[-3:]
    rows = out_refs[0].shape[0]
    heads = ws * cores
    some = tile // cores
    size = some // rows * heads
    my_z, my_w = place_ref[0] * z0s + place_ref[1], place_ref[2]
    for pair in range(ZS // 2):
        z = my_z ^ (2 * pair)
        run = other_run(my_w, z)

        def step(x, carry, pair=pair, z=z, runs=(0, 1)):
            for chunk in range(2):
                slot = z // 2 * 2 + chunk
                for array in range(arrays):
                    base = (chunk * arrays + array) * some * heads
                    for side in range(2):
                        at = 2 * pair + side
                        block = first_ref[x, at, array] if chunk == 0 else second_refs[at][x, array]
                        block = block.astype(F32)
                        for core in range(cores):
                            spot = pl.ds(base + runs[side] * cores + core, some, stride=heads)
                            wide[spot, :] = block[core * some : (core + 1) * some]
                    for row in range(rows):
                        to = pl.multiple_of((slot * xs + x) * size, size)
                        block = wide[pl.ds(base + row * size, size), :].astype(BF16)
                        out_refs[array][row, pl.ds(to, size), :] = block
            return carry

        for which in range(ws):

            @pl.when(run == which)
            def _(step=step, which=which):
                lax.fori_loop(0, xs, functools.partial(step, runs=(which, 1 - which)), 0)


def unpack(first, second, place, sizes, rows, after):
    ys, _, _, xs, ws, cores = sizes
    arrays, tile, feature = first.shape[-3:]
    width = ys * ZS * xs * tile // rows * ws
    return pl.pallas_call(
        lambda *refs: unpack_kernel(sizes, *refs),
        out_shape=[jax.ShapeDtypeStruct((rows, width, feature), BF16)] * arrays,
        grid=(ys,),
        in_specs=[SCALARS, ANY]
        + [pl.BlockSpec((xs, ZS, arrays, tile, feature), lambda i: (i, 0, 0, 0, 0))]
        + [pl.BlockSpec((xs, arrays, tile, feature), lambda i: (i, 0, 0, 0))] * ZS,
        out_specs=[pl.BlockSpec((rows, width // ys, feature), lambda i: (0, i, 0))] * arrays,
        scratch_shapes=[pltpu.VMEM((2 * arrays * tile * ws, feature), F32)],
        compiler_params=pltpu.CompilerParams(vmem_limit_bytes=ALL),
        name="unpack",
    )(place, after, first, *second)


def z_in(pieces):
    return [pieces[0]] + [
        lax.ppermute(
            pieces[k], ("z1", "z0"), [(z, (z + k) % ZS) for z in range(ZS)]
        )
        for k in range(1, ZS)
    ]


def z_out(pieces):
    def pairs(shift):
        made = []
        for z in range(ZS):
            for w in range(2):
                to = (w + (z in (0, ZS - 1))) % 2
                made.append((z * 2 + w, (z ^ shift) * 2 + to))
        return made

    return [lax.ppermute(pieces[k], ("z1", "z0", "w"), pairs(k)) for k in range(ZS)]


def shards(*arrays):
    sizes = tuple(lax.axis_size(name) for name in FINE)
    ys, z1s, z0s, xs, ws, cores = sizes
    rows, columns, _, feature = arrays[0].shape
    owners = ys * z1s * z0s * xs
    inner = columns // (owners * ws * cores)
    arrays = [a.reshape(rows, ws * cores, ys, ZS, xs, inner, feature) for a in arrays]
    place = jnp.stack([lax.axis_index(name) for name in ("z1", "z0", "w")]).astype(jnp.int32)

    def flat(piece):
        return piece.reshape(*piece.shape[:-3], rows * inner, feature)

    def across(whole, names):
        return lax.all_to_all(whole, names, 0, 0, tiled=True)

    packed = [flat(p) for p in pack(arrays, place, sizes, 0, True)]
    second = flat(pack(arrays, place, sizes, 1, False, packed[:1])[0])
    first = z_in(packed)
    pieces = parts(across(second, NEAR), hold(first[1:]), [2])
    second = z_in(pieces)
    first = across(join(first, pieces[2]), NEAR)

    done = attend([first], place, sizes, True, hold(second[2:3]))
    first = z_out(done)
    second = attend(second, place, sizes, False, done[0])[0]
    pieces = parts(across(second, ("y", "x")), hold(first), [1, 2])
    second = z_out(pieces)
    first = across(join(first, pieces[1]), ("y", "x"))

    results = unpack(first, second, place, sizes, rows, hold(second[1:3]))
    return tuple(r.reshape(rows, columns // (ws * cores), ws * cores, feature) for r in results)


def solution(mesh):
    fine = Mesh(mesh.devices.reshape(SIZES), FINE)
    row, head = FINE[:4], FINE[4:]
    spec_in = P(row, None, head, None)
    spec_out = P(row, head, None, None)
    return jax.shard_map(
        shards, mesh=fine, in_specs=(spec_in,) * 4, out_specs=(spec_out,) * 4, check_vma=False
    )
```

```python
import functools

import jax
import jax.numpy as jnp
from jax import lax
from jax.experimental import pallas as pl
from jax.experimental.pallas import tpu as pltpu
from jax.sharding import Mesh, PartitionSpec as P

FINE = ("y", "z1", "z0", "x", "w", "core")
SIZES = (4, 2, 2, 4, 2, 2)
NEAR = ("y", "x", "core")
LAST = (((1,), (1,)), ((), ()))
FIRST = (((0,), (0,)), ((), ()))
F32 = jnp.float32
BF16 = jnp.bfloat16
LIMIT = 24 * 2**20
SMALL = 6 * 2**20
ALL = 58 * 2**20
LOG2E = 1.4426950408889634
ANY = pl.BlockSpec(memory_space=pl.ANY)
FAR = pl.BlockSpec(memory_space=pltpu.HBM)
WHOLE = pl.BlockSpec(memory_space=pltpu.VMEM)
SCALARS = pl.BlockSpec(memory_space=pltpu.SMEM)
ZS = 4


def other_run(w, z):
    return (w + jnp.where((z == 0) | (z == ZS - 1), 1, 0)) % 2


def dot(a, b, dims):
    return lax.dot_general(a, b, dims, preferred_element_type=F32)


def attend_column(query, key, value, cotangent):
    half = query.shape[0] // 2
    scale = query.shape[-1] ** (-0.5)
    causal = lax.broadcasted_iota(jnp.int32, (half, half), 0) <= lax.broadcasted_iota(
        jnp.int32, (half, half), 1
    )
    lows, grads = [], []
    for at in range(2):
        mine, keys = slice(at * half, (at + 1) * half), slice(0, (at + 1) * half)
        scores = dot(key[keys], query[mine], LAST) * (scale * LOG2E)
        grad_weights = dot(value[keys], cotangent[mine], LAST)
        diagonal = jnp.where(causal, scores[mine], -jnp.inf)
        scores = jnp.concatenate([scores[:half], diagonal], 0) if at else diagonal
        raw = jnp.exp2(scores - jnp.max(scores, axis=0, keepdims=True))
        weights = raw * (1.0 / jnp.sum(raw, axis=0, keepdims=True))
        dots = jnp.sum(weights * grad_weights, axis=0, keepdims=True)
        lows.append(weights.astype(BF16))
        grads.append(((grad_weights - dots) * (weights * scale)).astype(BF16))

    def to_queries(parts, other):
        return jnp.concatenate(
            [dot(parts[0], other[:half], FIRST), dot(parts[1], other, FIRST)], axis=0
        )

    def to_keys(parts, other):
        upper = jnp.concatenate([parts[0], jnp.zeros((half, half), BF16)], axis=0)
        both = jnp.concatenate([upper, parts[1]], axis=1)
        return jnp.dot(both, other, preferred_element_type=F32)

    return (
        to_queries(lows, value),
        to_queries(grads, key),
        to_keys(grads, query),
        to_keys(lows, cotangent),
    )


def sending(made, out_refs, split, shift, sems):
    to = out_refs[shift] if split else out_refs[0].at[:, shift]
    copy = pltpu.make_async_copy(made.at[shift], to, sems.at[shift])
    copy.start()
    return copy


def pack_kernel(sizes, chunk, split, place_ref, *refs):
    ys, _, z0s, xs, _, cores = sizes
    *refs, held, made, sems, out_sems = refs
    far_refs, out_refs = refs[:4], refs[4 + (not split) :]
    rows = far_refs[0].shape[0]
    my_z, my_w = place_ref[0] * z0s + place_ref[1], place_ref[2]
    copies, sent = [], []
    for shift in range(ZS):
        z = (my_z + shift) % ZS
        quarter, slot = other_run(my_w, z) * cores, z // 2 * 2 + chunk
        for array, ref in enumerate(far_refs):
            copy = pltpu.make_async_copy(
                ref.at[:, pl.ds(quarter, cores), :, slot],
                held.at[shift, array],
                sems.at[shift, array],
            )
            copy.start()
            copies.append(copy)
    for shift in range(ZS):
        for copy in copies[shift * 4 : shift * 4 + 4]:
            copy.wait()

        def step(y, carry, shift=shift):
            for x in range(xs):
                for core in range(cores):
                    for array in range(4):
                        for row in range(rows):
                            to = (y * xs + x) * cores + core
                            made[shift, to, array, row] = held[shift, array, row, core, y, x]
            return carry

        lax.fori_loop(0, ys, step, 0)
        sent.append(sending(made, out_refs, split, shift, out_sems))
    for copy in sent:
        copy.wait()


def pack(arrays, place, sizes, chunk, split, after=()):
    ys, _, _, xs, _, cores = sizes
    rows, _, _, _, _, inner, feature = arrays[0].shape
    first, tail = ys * xs * cores, (len(arrays), rows, inner, feature)
    if split:
        shapes = [jax.ShapeDtypeStruct((first, *tail), BF16)] * ZS
    else:
        shapes = [jax.ShapeDtypeStruct((first, ZS, *tail), BF16)]
    return pl.pallas_call(
        lambda *refs: pack_kernel(sizes, chunk, split, *refs),
        out_shape=shapes,
        in_specs=[SCALARS] + [FAR] * 4 + [ANY] * len(after),
        out_specs=[FAR] * len(shapes),
        scratch_shapes=[
            pltpu.VMEM((ZS, 4, rows, cores, ys, xs, inner, feature), BF16),
            pltpu.VMEM((ZS, first, *tail), BF16),
            pltpu.SemaphoreType.DMA((ZS, 4)),
            pltpu.SemaphoreType.DMA((ZS,)),
        ],
        compiler_params=pltpu.CompilerParams(vmem_limit_bytes=ALL),
        name="pack",
    )(place, *arrays, *after)


def attend_kernel(sizes, pieces, split, place_ref, *refs):
    ys, _, z0s, xs, _, cores = sizes
    in_refs, refs = refs[:pieces], refs[pieces + 1 :]
    *out_refs, wide_in, wide_out, made, out_sems = refs
    sent = []
    sources = in_refs[0].shape[0]
    arrays, tile, feature = in_refs[0].shape[-3:]
    inner = tile // 4
    rows = ys * ZS * xs * 4
    my_z = place_ref[0] * z0s + place_ref[1]

    for shift in range(ZS):
        z = (my_z - shift + ZS) % ZS

        def widen(at, carry, shift=shift, z=z):
            y, x = at // xs, at % xs
            start = ((y * ZS + z) * xs + x) * tile
            for core in range(cores):
                for array in range(arrays):
                    source = at * cores + core
                    if pieces == 1:
                        block = in_refs[0][source, shift, array]
                    else:
                        block = in_refs[shift][source, array]
                    to = pl.multiple_of(core * rows * inner + start, tile)
                    wide_in[array, pl.ds(to, tile), :] = block.astype(F32)
            return carry

        lax.fori_loop(0, sources // cores, widen, 0, unroll=2)

    def column(core, carry):
        for place in range(inner):
            spot = pl.ds(core * rows * inner + place, rows, stride=inner)
            block = [wide_in[array, spot, :].astype(BF16) for array in range(arrays)]
            for array, result in enumerate(attend_column(*block)):
                wide_out[array, spot, :] = result
        return carry

    lax.fori_loop(0, cores, column, 0)

    for shift in range(ZS):
        z = my_z ^ shift

        def narrow(at, carry, shift=shift, z=z):
            y, x = at // xs, at % xs
            start = ((y * ZS + z) * xs + x) * tile
            for array in range(arrays):
                for core in range(cores):
                    spot = pl.ds(pl.multiple_of(core * rows * inner + start, tile), tile)
                    block = wide_out[array, spot, :].astype(BF16)
                    made[shift, at, array, core * tile : (core + 1) * tile] = block
            return carry

        lax.fori_loop(0, ys * xs, narrow, 0, unroll=2)
        sent.append(sending(made, out_refs, split, shift, out_sems))
    for copy in sent:
        copy.wait()


def attend(pieces, place, sizes, split, after):
    ys, _, _, xs, _, cores = sizes
    arrays, tile, feature = pieces[0].shape[-3:]
    rows = ys * ZS * xs * 4
    columns = tile // 4 * cores
    tail = (arrays, tile * cores, feature)
    if split:
        shapes = [jax.ShapeDtypeStruct((ys * xs, *tail), BF16)] * ZS
    else:
        shapes = [jax.ShapeDtypeStruct((ys * xs, ZS, *tail), BF16)]
    return pl.pallas_call(
        lambda *refs: attend_kernel(sizes, len(pieces), split, *refs),
        out_shape=shapes,
        in_specs=[SCALARS] + [WHOLE] * len(pieces) + [ANY],
        out_specs=[FAR] * len(shapes),
        scratch_shapes=[
            pltpu.VMEM((arrays, rows * columns + 8, feature), F32),
            pltpu.VMEM((arrays, rows * columns + 8, feature), F32),
            pltpu.VMEM((ZS, ys * xs, *tail), BF16),
            pltpu.SemaphoreType.DMA((ZS,)),
        ],
        compiler_params=pltpu.CompilerParams(vmem_limit_bytes=LIMIT),
        cost_estimate=pl.CostEstimate(flops=0, bytes_accessed=0, transcendentals=0),
        name="attend",
    )(place, *pieces, after)


def relay(sources, targets, held, sems):
    first = held.shape[1]
    cuts = [0, first // 2, first] if first > 1 else [0, first]
    steps = []
    for at, (source, target) in enumerate(zip(sources, targets)):
        for part_at in range(len(cuts) - 1):
            some = slice(cuts[part_at], cuts[part_at + 1])
            spot, sem = held.at[at, some], sems.at[at, part_at]
            into = pltpu.make_async_copy(source.at[some], spot, sem.at[0])
            out = pltpu.make_async_copy(spot, target.at[some], sem.at[1])
            into.start()
            steps.append((into, out))
    for into, out in steps:
        into.wait()
        out.start()
    for _, out in steps:
        out.wait()


def relay_scratch(count, shape):
    return [pltpu.VMEM((count, *shape), BF16), pltpu.SemaphoreType.DMA((count, 2, 2))]


def join_kernel(*refs):
    *in_refs, _, out_ref, held, sems = refs
    relay(in_refs, [out_ref.at[:, k] for k in range(len(in_refs))], held, sems)


def join(pieces, after):
    first, *tail = pieces[0].shape
    count = len(pieces)
    return pl.pallas_call(
        join_kernel,
        out_shape=jax.ShapeDtypeStruct((first, count, *tail), BF16),
        in_specs=[ANY] * (count + 1),
        out_specs=ANY,
        scratch_shapes=relay_scratch(count, (first, *tail)),
        compiler_params=pltpu.CompilerParams(vmem_limit_bytes=SMALL),
        name="join",
    )(*pieces, after)


def part_kernel(picks, in_ref, _, *refs):
    *out_refs, held, sems = refs
    relay([in_ref.at[:, pick] for pick in picks], out_refs, held, sems)


def part(joined, after, picks):
    first, _, *tail = joined.shape
    count = len(picks)
    return pl.pallas_call(
        lambda *refs: part_kernel(picks, *refs),
        out_shape=[jax.ShapeDtypeStruct((first, *tail), BF16)] * count,
        in_specs=[ANY] * 2,
        out_specs=[ANY] * count,
        scratch_shapes=relay_scratch(count, (first, *tail)),
        compiler_params=pltpu.CompilerParams(vmem_limit_bytes=SMALL),
        name="part",
    )(joined, after)


def parts(joined, after, early):
    late = [k for k in range(ZS) if k not in early]
    made = part(joined, after, early)
    found = dict(zip(early, made)) | dict(zip(late, part(joined, made[0], late)))
    return [found[k] for k in range(ZS)]


def hold_kernel(*refs):
    refs[-1][...] = jnp.zeros_like(refs[-1])


def hold(waited, flops=10**12):
    return pl.pallas_call(
        hold_kernel,
        out_shape=jax.ShapeDtypeStruct((8, 128), F32),
        in_specs=[ANY] * len(waited),
        out_specs=WHOLE,
        compiler_params=pltpu.CompilerParams(vmem_limit_bytes=SMALL),
        cost_estimate=pl.CostEstimate(flops=flops, bytes_accessed=4096, transcendentals=0),
        name="hold",
    )(*waited)


def unpack_kernel(sizes, place_ref, _, first_ref, *refs):
    _, _, z0s, xs, ws, cores = sizes
    second_refs, refs = refs[:ZS], refs[ZS:]
    *out_refs, wide = refs
    arrays, tile, feature = first_ref.shape[-3:]
    rows = out_refs[0].shape[0]
    heads = ws * cores
    some = tile // cores
    size = some // rows * heads
    my_z, my_w = place_ref[0] * z0s + place_ref[1], place_ref[2]
    for pair in range(ZS // 2):
        z = my_z ^ (2 * pair)
        run = other_run(my_w, z)

        def step(x, carry, pair=pair, z=z, runs=(0, 1)):
            for chunk in range(2):
                slot = z // 2 * 2 + chunk
                for array in range(arrays):
                    base = (chunk * arrays + array) * some * heads
                    for side in range(2):
                        at = 2 * pair + side
                        block = first_ref[x, at, array] if chunk == 0 else second_refs[at][x, array]
                        block = block.astype(F32)
                        for core in range(cores):
                            spot = pl.ds(base + runs[side] * cores + core, some, stride=heads)
                            wide[spot, :] = block[core * some : (core + 1) * some]
                    for row in range(rows):
                        to = pl.multiple_of((slot * xs + x) * size, size)
                        block = wide[pl.ds(base + row * size, size), :].astype(BF16)
                        out_refs[array][row, pl.ds(to, size), :] = block
            return carry

        for which in range(ws):

            @pl.when(run == which)
            def _(step=step, which=which):
                lax.fori_loop(0, xs, functools.partial(step, runs=(which, 1 - which)), 0)


def unpack(first, second, place, sizes, rows, after):
    ys, _, _, xs, ws, cores = sizes
    arrays, tile, feature = first.shape[-3:]
    width = ys * ZS * xs * tile // rows * ws
    return pl.pallas_call(
        lambda *refs: unpack_kernel(sizes, *refs),
        out_shape=[jax.ShapeDtypeStruct((rows, width, feature), BF16)] * arrays,
        grid=(ys,),
        in_specs=[SCALARS, ANY]
        + [pl.BlockSpec((xs, ZS, arrays, tile, feature), lambda i: (i, 0, 0, 0, 0))]
        + [pl.BlockSpec((xs, arrays, tile, feature), lambda i: (i, 0, 0, 0))] * ZS,
        out_specs=[pl.BlockSpec((rows, width // ys, feature), lambda i: (0, i, 0))] * arrays,
        scratch_shapes=[pltpu.VMEM((2 * arrays * tile * ws + 8, feature), F32)],
        compiler_params=pltpu.CompilerParams(vmem_limit_bytes=ALL),
        name="unpack",
    )(place, after, first, *second)


def z_in(pieces):
    return [pieces[0]] + [
        lax.ppermute(
            pieces[k], ("z1", "z0"), [(z, (z + k) % ZS) for z in range(ZS)]
        )
        for k in range(1, ZS)
    ]


def z_out(pieces):
    def pairs(shift):
        made = []
        for z in range(ZS):
            for w in range(2):
                to = (w + (z in (0, ZS - 1))) % 2
                made.append((z * 2 + w, (z ^ shift) * 2 + to))
        return made

    return [lax.ppermute(pieces[k], ("z1", "z0", "w"), pairs(k)) for k in range(ZS)]


def shards(*arrays):
    sizes = tuple(lax.axis_size(name) for name in FINE)
    ys, z1s, z0s, xs, ws, cores = sizes
    rows, columns, _, feature = arrays[0].shape
    owners = ys * z1s * z0s * xs
    inner = columns // (owners * ws * cores)
    arrays = [a.reshape(rows, ws * cores, ys, ZS, xs, inner, feature) for a in arrays]
    place = jnp.stack([lax.axis_index(name) for name in ("z1", "z0", "w")]).astype(jnp.int32)

    def flat(piece):
        return piece.reshape(*piece.shape[:-3], rows * inner, feature)

    def across(whole, names):
        return lax.all_to_all(whole, names, 0, 0, tiled=True)

    packed = [flat(p) for p in pack(arrays, place, sizes, 0, True)]
    second = flat(pack(arrays, place, sizes, 1, False, packed[:1])[0])
    first = z_in(packed)
    pieces = parts(across(second, NEAR), hold(first[1:]), [2])
    second = z_in(pieces)
    first = across(join(first, pieces[2]), NEAR)

    done = attend([first], place, sizes, True, hold(second[2:3]))
    first = z_out(done)
    second = attend(second, place, sizes, False, done[0])[0]
    pieces = parts(across(second, ("y", "x")), hold(first), [0, 3])
    second = z_out(pieces)
    first = across(join(first, pieces[0]), ("y", "x"))

    results = unpack(first, second, place, sizes, rows, hold([second[k] for k in [0, 3]]))
    return tuple(r.reshape(rows, columns // (ws * cores), ws * cores, feature) for r in results)


def solution(mesh):
    fine = Mesh(mesh.devices.reshape(SIZES), FINE)
    row, head = FINE[:4], FINE[4:]
    spec_in = P(row, None, head, None)
    spec_out = P(row, head, None, None)
    return jax.shard_map(
        shards, mesh=fine, in_specs=(spec_in,) * 4, out_specs=(spec_out,) * 4, check_vma=False
    )
```

```python
import functools

import jax
import jax.numpy as jnp
from jax import lax
from jax.experimental import pallas as pl
from jax.experimental.pallas import tpu as pltpu
from jax.sharding import Mesh, PartitionSpec as P

FINE = ("y", "z1", "z0", "x", "w", "core")
SIZES = (4, 2, 2, 4, 2, 2)
NEAR = ("y", "x", "core")
LAST = (((1,), (1,)), ((), ()))
FIRST = (((0,), (0,)), ((), ()))
F32 = jnp.float32
BF16 = jnp.bfloat16
LIMIT = 24 * 2**20
SMALL = 6 * 2**20
ALL = 58 * 2**20
LOG2E = 1.4426950408889634
ANY = pl.BlockSpec(memory_space=pl.ANY)
FAR = pl.BlockSpec(memory_space=pltpu.HBM)
WHOLE = pl.BlockSpec(memory_space=pltpu.VMEM)
SCALARS = pl.BlockSpec(memory_space=pltpu.SMEM)
ZS = 4


def other_run(w, z):
    return (w + jnp.where((z == 0) | (z == ZS - 1), 1, 0)) % 2


def dot(a, b, dims):
    return lax.dot_general(a, b, dims, preferred_element_type=F32)


def attend_column(query, key, value, cotangent):
    half = query.shape[0] // 2
    scale = query.shape[-1] ** (-0.5)
    causal = lax.broadcasted_iota(jnp.int32, (half, half), 0) <= lax.broadcasted_iota(
        jnp.int32, (half, half), 1
    )
    lows, grads = [], []
    for at in range(2):
        mine, keys = slice(at * half, (at + 1) * half), slice(0, (at + 1) * half)
        scores = dot(key[keys], query[mine], LAST) * (scale * LOG2E)
        grad_weights = dot(value[keys], cotangent[mine], LAST)
        diagonal = jnp.where(causal, scores[mine], -jnp.inf)
        scores = jnp.concatenate([scores[:half], diagonal], 0) if at else diagonal
        raw = jnp.exp2(scores - jnp.max(scores, axis=0, keepdims=True))
        weights = raw * (1.0 / jnp.sum(raw, axis=0, keepdims=True))
        dots = jnp.sum(weights * grad_weights, axis=0, keepdims=True)
        lows.append(weights.astype(BF16))
        grads.append(((grad_weights - dots) * (weights * scale)).astype(BF16))

    def to_queries(parts, other):
        return jnp.concatenate(
            [dot(parts[0], other[:half], FIRST), dot(parts[1], other, FIRST)], axis=0
        )

    def to_keys(parts, other):
        upper = jnp.concatenate([parts[0], jnp.zeros((half, half), BF16)], axis=0)
        both = jnp.concatenate([upper, parts[1]], axis=1)
        return jnp.dot(both, other, preferred_element_type=F32)

    return (
        to_queries(lows, value),
        to_queries(grads, key),
        to_keys(grads, query),
        to_keys(lows, cotangent),
    )


def sending(made, out_refs, split, shift, sems):
    to = out_refs[shift] if split else out_refs[0].at[:, shift]
    copy = pltpu.make_async_copy(made.at[shift], to, sems.at[shift])
    copy.start()
    return copy


def pack_kernel(sizes, chunk, split, place_ref, *refs):
    ys, _, z0s, xs, _, cores = sizes
    *refs, held, made, sems, out_sems = refs
    far_refs, out_refs = refs[:4], refs[4 + (not split) :]
    rows = far_refs[0].shape[0]
    my_z, my_w = place_ref[0] * z0s + place_ref[1], place_ref[2]
    copies, sent = [], []
    for shift in range(ZS):
        z = (my_z + shift) % ZS
        quarter, slot = other_run(my_w, z) * cores, z // 2 * 2 + chunk
        for array, ref in enumerate(far_refs):
            copy = pltpu.make_async_copy(
                ref.at[:, pl.ds(quarter, cores), :, slot],
                held.at[shift, array],
                sems.at[shift, array],
            )
            copy.start()
            copies.append(copy)
    for shift in range(ZS):
        for copy in copies[shift * 4 : shift * 4 + 4]:
            copy.wait()

        def step(y, carry, shift=shift):
            for x in range(xs):
                for core in range(cores):
                    for array in range(4):
                        for row in range(rows):
                            to = (y * xs + x) * cores + core
                            made[shift, to, array, row] = held[shift, array, row, core, y, x]
            return carry

        lax.fori_loop(0, ys, step, 0)
        sent.append(sending(made, out_refs, split, shift, out_sems))
    for copy in sent:
        copy.wait()


def pack(arrays, place, sizes, chunk, split, after=()):
    ys, _, _, xs, _, cores = sizes
    rows, _, _, _, _, inner, feature = arrays[0].shape
    first, tail = ys * xs * cores, (len(arrays), rows, inner, feature)
    if split:
        shapes = [jax.ShapeDtypeStruct((first, *tail), BF16)] * ZS
    else:
        shapes = [jax.ShapeDtypeStruct((first, ZS, *tail), BF16)]
    return pl.pallas_call(
        lambda *refs: pack_kernel(sizes, chunk, split, *refs),
        out_shape=shapes,
        in_specs=[SCALARS] + [FAR] * 4 + [ANY] * len(after),
        out_specs=[FAR] * len(shapes),
        scratch_shapes=[
            pltpu.VMEM((ZS, 4, rows, cores, ys, xs, inner, feature), BF16),
            pltpu.VMEM((ZS, first, *tail), BF16),
            pltpu.SemaphoreType.DMA((ZS, 4)),
            pltpu.SemaphoreType.DMA((ZS,)),
        ],
        compiler_params=pltpu.CompilerParams(vmem_limit_bytes=ALL),
        name="pack",
    )(place, *arrays, *after)


def attend_kernel(sizes, pieces, split, place_ref, *refs):
    ys, _, z0s, xs, _, cores = sizes
    in_refs, refs = refs[:pieces], refs[pieces + 1 :]
    *out_refs, wide_in, wide_out, made, out_sems = refs
    sent = []
    sources = in_refs[0].shape[0]
    arrays, tile, feature = in_refs[0].shape[-3:]
    inner = tile // 4
    rows = ys * ZS * xs * 4
    my_z = place_ref[0] * z0s + place_ref[1]

    for shift in range(ZS):
        z = (my_z - shift + ZS) % ZS

        def widen(at, carry, shift=shift, z=z):
            y, x = at // xs, at % xs
            start = ((y * ZS + z) * xs + x) * tile
            for core in range(cores):
                for array in range(arrays):
                    source = at * cores + core
                    if pieces == 1:
                        block = in_refs[0][source, shift, array]
                    else:
                        block = in_refs[shift][source, array]
                    to = pl.multiple_of(core * rows * inner + start, tile)
                    wide_in[array, pl.ds(to, tile), :] = block.astype(F32)
            return carry

        lax.fori_loop(0, sources // cores, widen, 0, unroll=2)

    def column(core, carry):
        for place in range(inner):
            spot = pl.ds(core * rows * inner + place, rows, stride=inner)
            block = [wide_in[array, spot, :].astype(BF16) for array in range(arrays)]
            for array, result in enumerate(attend_column(*block)):
                wide_out[array, spot, :] = result
        return carry

    lax.fori_loop(0, cores, column, 0)

    for shift in range(ZS):
        z = my_z ^ shift

        def narrow(at, carry, shift=shift, z=z):
            y, x = at // xs, at % xs
            start = ((y * ZS + z) * xs + x) * tile
            for array in range(arrays):
                for core in range(cores):
                    spot = pl.ds(pl.multiple_of(core * rows * inner + start, tile), tile)
                    block = wide_out[array, spot, :].astype(BF16)
                    made[shift, at, array, core * tile : (core + 1) * tile] = block
            return carry

        lax.fori_loop(0, ys * xs, narrow, 0, unroll=2)
        sent.append(sending(made, out_refs, split, shift, out_sems))
    for copy in sent:
        copy.wait()


def attend(pieces, place, sizes, split, after):
    ys, _, _, xs, _, cores = sizes
    arrays, tile, feature = pieces[0].shape[-3:]
    rows = ys * ZS * xs * 4
    columns = tile // 4 * cores
    tail = (arrays, tile * cores, feature)
    if split:
        shapes = [jax.ShapeDtypeStruct((ys * xs, *tail), BF16)] * ZS
    else:
        shapes = [jax.ShapeDtypeStruct((ys * xs, ZS, *tail), BF16)]
    return pl.pallas_call(
        lambda *refs: attend_kernel(sizes, len(pieces), split, *refs),
        out_shape=shapes,
        in_specs=[SCALARS] + [WHOLE] * len(pieces) + [ANY],
        out_specs=[FAR] * len(shapes),
        scratch_shapes=[
            pltpu.VMEM((arrays, rows * columns + 8, feature), F32),
            pltpu.VMEM((arrays, rows * columns + 8, feature), F32),
            pltpu.VMEM((ZS, ys * xs, *tail), BF16),
            pltpu.SemaphoreType.DMA((ZS,)),
        ],
        compiler_params=pltpu.CompilerParams(vmem_limit_bytes=LIMIT),
        cost_estimate=pl.CostEstimate(flops=0, bytes_accessed=0, transcendentals=0),
        name="attend",
    )(place, *pieces, after)


def relay(sources, targets, held, sems):
    first = held.shape[1]
    cuts = [0, first // 2, first] if first > 1 else [0, first]
    steps = []
    for at, (source, target) in enumerate(zip(sources, targets)):
        for part_at in range(len(cuts) - 1):
            some = slice(cuts[part_at], cuts[part_at + 1])
            spot, sem = held.at[at, some], sems.at[at, part_at]
            into = pltpu.make_async_copy(source.at[some], spot, sem.at[0])
            out = pltpu.make_async_copy(spot, target.at[some], sem.at[1])
            into.start()
            steps.append((into, out))
    for into, out in steps:
        into.wait()
        out.start()
    for _, out in steps:
        out.wait()


def relay_scratch(count, shape):
    return [pltpu.VMEM((count, *shape), BF16), pltpu.SemaphoreType.DMA((count, 2, 2))]


def join_kernel(*refs):
    *in_refs, _, out_ref, held, sems = refs
    relay(in_refs, [out_ref.at[:, k] for k in range(len(in_refs))], held, sems)


def join(pieces, after):
    first, *tail = pieces[0].shape
    count = len(pieces)
    return pl.pallas_call(
        join_kernel,
        out_shape=jax.ShapeDtypeStruct((first, count, *tail), BF16),
        in_specs=[ANY] * (count + 1),
        out_specs=ANY,
        scratch_shapes=relay_scratch(count, (first, *tail)),
        compiler_params=pltpu.CompilerParams(vmem_limit_bytes=SMALL),
        name="join",
    )(*pieces, after)


def part_kernel(picks, in_ref, _, *refs):
    *out_refs, held, sems = refs
    relay([in_ref.at[:, pick] for pick in picks], out_refs, held, sems)


def part(joined, after, picks):
    first, _, *tail = joined.shape
    count = len(picks)
    return pl.pallas_call(
        lambda *refs: part_kernel(picks, *refs),
        out_shape=[jax.ShapeDtypeStruct((first, *tail), BF16)] * count,
        in_specs=[ANY] * 2,
        out_specs=[ANY] * count,
        scratch_shapes=relay_scratch(count, (first, *tail)),
        compiler_params=pltpu.CompilerParams(vmem_limit_bytes=SMALL),
        name="part",
    )(joined, after)


def parts(joined, after, early):
    late = [k for k in range(ZS) if k not in early]
    made = part(joined, after, early)
    found = dict(zip(early, made)) | dict(zip(late, part(joined, made[0], late)))
    return [found[k] for k in range(ZS)]


def hold_kernel(*refs):
    refs[-1][...] = jnp.zeros_like(refs[-1])


def hold(waited, flops=10**12):
    return pl.pallas_call(
        hold_kernel,
        out_shape=jax.ShapeDtypeStruct((8, 128), F32),
        in_specs=[ANY] * len(waited),
        out_specs=WHOLE,
        compiler_params=pltpu.CompilerParams(vmem_limit_bytes=SMALL),
        cost_estimate=pl.CostEstimate(flops=flops, bytes_accessed=4096, transcendentals=0),
        name="hold",
    )(*waited)


def unpack_kernel(sizes, place_ref, _, first_ref, *refs):
    _, _, z0s, xs, ws, cores = sizes
    second_refs, refs = refs[:ZS], refs[ZS:]
    *out_refs, wide = refs
    arrays, tile, feature = first_ref.shape[-3:]
    rows = out_refs[0].shape[0]
    heads = ws * cores
    some = tile // cores
    size = some // rows * heads
    my_z, my_w = place_ref[0] * z0s + place_ref[1], place_ref[2]
    for pair in range(ZS // 2):
        z = my_z ^ (2 * pair)
        run = other_run(my_w, z)

        def step(x, carry, pair=pair, z=z, runs=(0, 1)):
            for chunk in range(2):
                slot = z // 2 * 2 + chunk
                for array in range(arrays):
                    base = (chunk * arrays + array) * some * heads
                    for side in range(2):
                        at = 2 * pair + side
                        block = first_ref[x, at, array] if chunk == 0 else second_refs[at][x, array]
                        block = block.astype(F32)
                        for core in range(cores):
                            spot = pl.ds(base + runs[side] * cores + core, some, stride=heads)
                            wide[spot, :] = block[core * some : (core + 1) * some]
                    for row in range(rows):
                        to = pl.multiple_of((slot * xs + x) * size, size)
                        block = wide[pl.ds(base + row * size, size), :].astype(BF16)
                        out_refs[array][row, pl.ds(to, size), :] = block
            return carry

        for which in range(ws):

            @pl.when(run == which)
            def _(step=step, which=which):
                lax.fori_loop(0, xs, functools.partial(step, runs=(which, 1 - which)), 0)


def unpack(first, second, place, sizes, rows, after):
    ys, _, _, xs, ws, cores = sizes
    arrays, tile, feature = first.shape[-3:]
    width = ys * ZS * xs * tile // rows * ws
    return pl.pallas_call(
        lambda *refs: unpack_kernel(sizes, *refs),
        out_shape=[jax.ShapeDtypeStruct((rows, width, feature), BF16)] * arrays,
        grid=(ys,),
        in_specs=[SCALARS, ANY]
        + [pl.BlockSpec((xs, ZS, arrays, tile, feature), lambda i: (i, 0, 0, 0, 0))]
        + [pl.BlockSpec((xs, arrays, tile, feature), lambda i: (i, 0, 0, 0))] * ZS,
        out_specs=[pl.BlockSpec((rows, width // ys, feature), lambda i: (0, i, 0))] * arrays,
        scratch_shapes=[pltpu.VMEM((2 * arrays * tile * ws + 8, feature), F32)],
        compiler_params=pltpu.CompilerParams(vmem_limit_bytes=ALL),
        name="unpack",
    )(place, after, first, *second)


def z_in(pieces):
    return [pieces[0]] + [
        lax.ppermute(
            pieces[k], ("z1", "z0"), [(z, (z + k) % ZS) for z in range(ZS)]
        )
        for k in range(1, ZS)
    ]


def z_out(pieces):
    def pairs(shift):
        made = []
        for z in range(ZS):
            for w in range(2):
                to = (w + (z in (0, ZS - 1))) % 2
                made.append((z * 2 + w, (z ^ shift) * 2 + to))
        return made

    return [lax.ppermute(pieces[k], ("z1", "z0", "w"), pairs(k)) for k in range(ZS)]


def shards(*arrays):
    sizes = tuple(lax.axis_size(name) for name in FINE)
    ys, z1s, z0s, xs, ws, cores = sizes
    rows, columns, _, feature = arrays[0].shape
    owners = ys * z1s * z0s * xs
    inner = columns // (owners * ws * cores)
    arrays = [a.reshape(rows, ws * cores, ys, ZS, xs, inner, feature) for a in arrays]
    place = jnp.stack([lax.axis_index(name) for name in ("z1", "z0", "w")]).astype(jnp.int32)

    def flat(piece):
        return piece.reshape(*piece.shape[:-3], rows * inner, feature)

    def across(whole, names):
        return lax.all_to_all(whole, names, 0, 0, tiled=True)

    packed = [flat(p) for p in pack(arrays, place, sizes, 0, True)]
    second = flat(pack(arrays, place, sizes, 1, False, packed[:1])[0])
    first = z_in(packed)
    pieces = parts(across(second, NEAR), hold(first[1:]), [2])
    second = z_in(pieces)
    first = across(join(first, pieces[2]), NEAR)

    done = attend([first], place, sizes, True, hold(second[2:3]))
    first = z_out(done)
    second = attend(second, place, sizes, False, done[0])[0]
    pieces = parts(across(second, ("y", "x")), hold([first[0], first[1], first[3]]), [0, 3])
    second = z_out(pieces)
    first = across(join(first, pieces[0]), ("y", "x"))

    results = unpack(first, second, place, sizes, rows, hold([second[k] for k in [0, 3]]))
    return tuple(r.reshape(rows, columns // (ws * cores), ws * cores, feature) for r in results)


def solution(mesh):
    fine = Mesh(mesh.devices.reshape(SIZES), FINE)
    row, head = FINE[:4], FINE[4:]
    spec_in = P(row, None, head, None)
    spec_out = P(row, head, None, None)
    return jax.shard_map(
        shards, mesh=fine, in_specs=(spec_in,) * 4, out_specs=(spec_out,) * 4, check_vma=False
    )
```
